32 devices in a mesh: lat: 4 (over x, core), lon: 8 (over z, y).
Axes of the slice: x: 2, y: 2, z: 4, core: 2. Of those that a mesh axis runs over, the one named last changes fastest.
Arguments:
- velocity: bfloat16 [2, 256, 384, 512], P(None, None, 'lon', 'lat'), may hold values from -16 to 16
- lon_metric: float32 [384, 512], P('lon', 'lat'), may hold values from 0.5 to 2
- lat_metric: float32 [384, 512], P('lon', 'lat'), may hold values from 0.5 to 2
- wet_index: int32 [196608], P(('lat', 'lon')), may hold values from 0 to 6143, as said below
- wet_count: int32 [32], P(('lat', 'lon')), may hold values from 3072 to 6144, as said below
Outputs:
- basis: bfloat16 [512, 196608], P(None, ('lat', 'lon'))
- r_factor: float32 [512, 512], replicated
The draws below stay inside these ranges and needn't reach their ends.
Inputs may be any that keep to these rules, and one draw needn't show every extreme that they name: `wet_index`: each device's 6144 entries are a permutation of its local cells 0 to 6143. `wet_count`: some device has all 6144 cells wet.
All inputs are finite; a program needn't handle non-finite values.
Results may differ from the reference program's by a relative error of at most 0.001.
The reference program's roundings to bfloat16 on the way (of `fields` and `snapshot`) count: a program that leaves them out, or rounds other values in their place, can miss the bound.
Values may be sent and summed in bfloat16 or wider, within the bound.
No kernel may reach another device: no remote copies, remote signals or barrier semaphores. Data moves between devices by JAX's collectives and lax.ppermute only.
A program may use at most 128 MiB of HBM per device.

```python
import math
import jax
import jax.numpy as jnp
from jax import lax

S = 256
CX = 48
CY = 128
CELLS = 6144
NX = 384
NY = 512
ROWS = 196608
N_LAT = 4
N_LON = 8


def draw_velocity(key, part):
    keyed = jax.random.fold_in(key, 3)
    key_base, key_amp, key_noise = jax.random.split(keyed, 3)
    position = jnp.arange(NY, dtype=jnp.float32) / max(NY - 1, 1)
    base_flow = jax.random.normal(key_base, (2, 1, NX, NY), jnp.float32)
    amplitude = jax.random.uniform(key_amp, (1, S, 1, 1), jnp.float32, 0.5, 1.5)
    anomaly = jax.random.normal(key_noise, (2, S, NX, NY), jnp.float32)
    lat_scale = 1.0 + 2.0 * position
    values = (base_flow * amplitude + anomaly) * lat_scale[None, None, None, :]
    return jnp.clip(values, -16.0, 16.0).astype(jnp.bfloat16)


def wet_plan(key):
    keyed = jax.random.fold_in(key, 7)
    key_count, key_full, key_perm = jax.random.split(keyed, 3)
    devices = ROWS // CELLS
    counts = jax.random.randint(key_count, (devices,), CELLS // 2, CELLS + 1)
    full_device = jax.random.randint(key_full, (), 0, devices)
    counts = jnp.where(jnp.arange(devices) == full_device, CELLS, counts).astype(jnp.int32)
    perm_keys = jax.random.split(key_perm, devices)
    orders = jax.vmap(lambda single: jax.random.permutation(single, CELLS))(perm_keys)
    return (counts, orders.reshape(-1).astype(jnp.int32))


def draw_wet_index(key, part):
    return wet_plan(key)[1]


def draw_wet_count(key, part):
    return wet_plan(key)[0]


def shard_levels(own_key, extent, shards, low, high):
    gain = 1.0
    for axis_at, shards_of in shards:
        draws = jax.random.uniform(jax.random.fold_in(jax.random.fold_in(own_key, 6), axis_at), (shards_of,), jnp.float32, low / len(shards), high / len(shards))
        gain = gain * jnp.repeat(jnp.exp(draws), extent[axis_at] // shards_of).reshape((-1,) + (1,) * (len(extent) - 1 - axis_at))
    return gain


def setup_inputs(seed: int = 0) -> dict:
    key_of = jax.random.split(jax.random.key(seed), 6)
    velocity = draw_velocity(jax.random.fold_in(key_of[5], 71), 0)
    lon_metric = jnp.clip(jnp.exp(math.log(2.0) - 1.3862944 * jax.random.uniform(key_of[1], (NX, NY), jnp.float32) ** shard_levels(key_of[1], (NX, NY), ((0, 8), (1, 4)), -0.2, 0.2)), 0.5, 2.0)
    lat_metric = jnp.clip(jnp.exp(math.log(2.0) - 1.3862944 * jax.random.uniform(key_of[2], (NX, NY), jnp.float32) ** shard_levels(key_of[2], (NX, NY), ((0, 8), (1, 4)), -0.2, 0.2)), 0.5, 2.0)
    wet_index = draw_wet_index(jax.random.fold_in(key_of[5], 71), 0)
    wet_count = draw_wet_count(jax.random.fold_in(key_of[5], 71), 0)
    return dict(velocity=velocity, lon_metric=lon_metric, lat_metric=lat_metric, wet_index=wet_index, wet_count=wet_count)


def one_day(pair, lon_metric, lat_metric):
    vel32 = pair.astype(jnp.float32)
    east_cell = jnp.roll(vel32, -1, axis=1)
    west_cell = jnp.roll(vel32, 1, axis=1)
    ghost_row = -vel32[:, ::-1, -1]
    above = jnp.concatenate([vel32[:, :, 1:], ghost_row[:, :, None]], axis=2)
    below = jnp.concatenate([jnp.zeros_like(vel32[:, :, :1]), vel32[:, :, :-1]], axis=2)
    across = 0.5 * lon_metric * (east_cell - west_cell)
    along = 0.5 * lat_metric * (above - below)
    zeta = across[1] - along[0]
    divergence = across[0] + along[1]
    return jnp.stack([zeta, divergence]).astype(jnp.bfloat16)

def reference(velocity, lon_metric, lat_metric, wet_index, wet_count):
    days = jnp.transpose(velocity, (1, 0, 2, 3))
    daily = lax.map(lambda pair: one_day(pair, lon_metric, lat_metric), days)
    fields = jnp.transpose(daily, (1, 0, 2, 3)).reshape(2 * S, NX, NY)
    devices = N_LAT * N_LON
    blocks = fields.reshape(2 * S, N_LON, CX, N_LAT, CY).transpose(0, 3, 1, 2, 4).reshape(2 * S, devices, CELLS)
    index_table = wet_index.reshape(devices, CELLS).astype(jnp.int32)
    picked = jnp.take_along_axis(blocks, index_table[None, :, :], axis=2)
    live = jnp.arange(CELLS, dtype=jnp.int32)[None, :] < wet_count[:, None]
    picked = jnp.where(live[None, :, :], picked, jnp.zeros_like(picked))
    snapshot = picked.reshape(2 * S, ROWS).T.astype(jnp.float32)
    ortho, triangle = jnp.linalg.qr(snapshot)
    signs = jnp.sign(jnp.diagonal(triangle))
    triangle = signs[:, None] * triangle
    ortho = ortho * signs[None, :]
    scale = math.sqrt(ROWS)
    basis = (ortho.T * scale).astype(jnp.bfloat16)
    return (basis, triangle / scale)
```

```python
import functools
import math

import jax
import jax.numpy as jnp
from jax import lax
from jax.experimental import pallas as pl
from jax.experimental.pallas import tpu as pltpu
from jax.sharding import PartitionSpec as P

F32 = jnp.float32
BF16 = jnp.bfloat16
MB = 1 << 20
NN = (((1,), (0,)), ((), ()))
NT = (((1,), (1,)), ((), ()))
TN = (((0,), (0,)), ((), ()))


def iota(shape, dim):
    return lax.broadcasted_iota(jnp.int32, shape, dim)


def relayout_kernel(half, v_ref, out_ref, south_ref, north_ref, fold_ref, wide):
    fields, days, width_x, width_y = v_ref.shape
    lane = iota((16, width_y), 1)
    for f in range(fields):
        wide[f] = v_ref[f].astype(F32).reshape(days * width_x, width_y)
    for d in range(0, days, 16):
        south = jnp.zeros((16, width_y), F32)
        north = jnp.zeros((16, width_y), F32)
        fold = jnp.zeros((16, width_y), F32)
        for f in range(fields):
            for x in range(width_x):
                piece = wide[f, pl.ds(d * width_x + x, 16, stride=width_x), :]
                out_ref[f, x, d : d + 16, :] = piece.astype(BF16)
                at = f * half + x
                turned = pltpu.roll(piece, at + 1, 1)
                north = jnp.where(lane == at, turned, north)
                south = jnp.where(lane == at + 1, turned, south)
                back = f * half + width_x - x
                fold = jnp.where(lane == back, pltpu.roll(piece, back + 1, 1), fold)
        south_ref[d : d + 16, :] = south.astype(BF16)
        north_ref[d : d + 16, :] = north.astype(BF16)
        fold_ref[d : d + 16, :] = -fold.astype(BF16)


def relayout(velocity):
    fields, days, width_x, width_y = velocity.shape
    step = 32
    edge = jax.ShapeDtypeStruct((days, width_y), BF16)
    edge_spec = pl.BlockSpec((step, width_y), lambda i: (i, 0))
    return pl.pallas_call(
        functools.partial(relayout_kernel, width_y // 2),
        grid=(days // step,),
        in_specs=[pl.BlockSpec((fields, step, width_x, width_y), lambda i: (0, i, 0, 0))],
        out_specs=[
            pl.BlockSpec((fields, width_x, step, width_y), lambda i: (0, 0, i, 0)),
            edge_spec,
            edge_spec,
            edge_spec,
        ],
        out_shape=[
            jax.ShapeDtypeStruct((fields, width_x, days, width_y), BF16),
            edge,
            edge,
            edge,
        ],
        scratch_shapes=[pltpu.VMEM((fields, step * width_x, width_y), F32)],
        compiler_params=pltpu.CompilerParams(vmem_limit_bytes=40 * MB),
        name="relayout",
    )(velocity)


def wet_metrics_kernel(index_ref, count_ref, lon_ref, lat_ref, lon_out, lat_out):
    width_x, width_y = lon_ref.shape
    cells = index_ref.shape[1]
    index = index_ref[...]
    place = iota(index.shape, 1)
    wet = place < count_ref[0]
    row = jnp.where(wet, index // width_y, -1)
    col = index % width_y
    pick_x = jnp.where(iota((width_x, cells), 0) == row, 1.0, 0.0).astype(BF16)
    pick_y = jnp.where(iota((width_y, cells), 0) == col, 1.0, 0.0).astype(BF16)
    mask = lax.dot_general(pick_x, pick_y, NT, preferred_element_type=F32)
    lon_out[...] = 0.5 * lon_ref[...] * mask
    lat_out[...] = 0.5 * lat_ref[...] * mask


def wet_metrics(wet_index, wet_count, lon_metric, lat_metric):
    vmem = pl.BlockSpec(memory_space=pltpu.VMEM)
    return pl.pallas_call(
        wet_metrics_kernel,
        in_specs=[vmem, pl.BlockSpec(memory_space=pltpu.SMEM), vmem, vmem],
        out_specs=[vmem, vmem],
        out_shape=[jax.ShapeDtypeStruct(lon_metric.shape, F32)] * 2,
        compiler_params=pltpu.CompilerParams(vmem_limit_bytes=40 * MB),
        name="wet_metrics",
    )(wet_index.reshape(1, -1), wet_count, lon_metric, lat_metric)


def stencil_kernel(
    v_ref, left_ref, right_ref, west_ref, east_ref, south_ref, north_ref, fold_ref,
    lon_ref, lat_ref, fields_ref, gram_ref, total,
):
    step, steps = pl.program_id(0), pl.num_programs(0)
    _, group, days, width_y = v_ref.shape
    half = width_y // 2
    wide = 2 * width_y

    k = iota((wide, wide), 0)
    n = iota((wide, wide), 1)
    same = k // width_y == n // width_y
    diff = jnp.where(same & (k == n + 1), 1.0, 0.0) - jnp.where(same & (k == n - 1), 1.0, 0.0)
    diff = diff.astype(BF16)
    field = n // width_y
    lane = n % width_y
    sign = jnp.where(lane == 0, -1.0, 1.0)
    aim = jnp.where(
        lane == 0, k - field * half, jnp.where(lane == width_y - 1, k - width_y - field * half - 1, -1)
    )
    rim = jnp.concatenate([south_ref[...], north_ref[...] + fold_ref[...]], axis=1)
    first = step == 0
    last = step == steps - 1

    def column(f, g):
        if g < 0:
            return jnp.where(first, west_ref[f], left_ref[f, 0])
        if g >= group:
            return jnp.where(last, east_ref[f], right_ref[f, 0])
        return v_ref[f, g]

    for g in range(group):
        x = step * group + g
        here = jnp.concatenate([v_ref[0, g], v_ref[1, g]], axis=1)
        reach = jnp.where(aim == x, sign, 0.0).astype(BF16)
        along = lax.dot_general(here, diff, NN, preferred_element_type=F32)
        along = along + lax.dot_general(rim, reach, NN, preferred_element_type=F32)
        lon = lon_ref[pl.ds(x, 1), :]
        lat = lat_ref[pl.ds(x, 1), :]
        across_u = column(0, g + 1).astype(F32) - column(0, g - 1).astype(F32)
        across_v = column(1, g + 1).astype(F32) - column(1, g - 1).astype(F32)
        zeta = lon * across_v - lat * along[:, :width_y]
        divergence = lon * across_u + lat * along[:, width_y:]
        fields_ref[:days, g * width_y : (g + 1) * width_y] = zeta.astype(BF16)
        fields_ref[days:, g * width_y : (g + 1) * width_y] = divergence.astype(BF16)

    upper = lax.dot_general(
        fields_ref[:days, :], fields_ref[...], NT, preferred_element_type=F32
    )
    lower = lax.dot_general(
        fields_ref[days:, :], fields_ref[days:, :], NT, preferred_element_type=F32
    )

    @pl.when(first)
    def _():
        total[:days, :] = upper
        total[days:, days:] = lower

    @pl.when(jnp.logical_not(first))
    def _():
        total[:days, :] += upper
        total[days:, days:] += lower

    @pl.when(last)
    def _():
        size = gram_ref.shape[1]
        at = 0
        for i in range(2 * days // size):
            for j in range(i, 2 * days // size):
                gram_ref[at] = total[i * size : (i + 1) * size, j * size : (j + 1) * size]
                at += 1


def stencil(moved, west, east, south, north, fold, lon, lat, size):
    _, width_x, days, width_y = moved.shape
    group = next(g for g in (8, 6, 4, 3, 2, 1) if width_x % g == 0)
    count = 2 * days // size
    blocks = count * (count + 1) // 2
    rim_spec = pl.BlockSpec((days, width_y), lambda i: (0, 0))
    side_spec = pl.BlockSpec((2, days, width_y), lambda i: (0, 0, 0))
    metric_spec = pl.BlockSpec((width_x, width_y), lambda i: (0, 0))
    return pl.pallas_call(
        stencil_kernel,
        grid=(width_x // group,),
        in_specs=[
            pl.BlockSpec((2, group, days, width_y), lambda i: (0, i, 0, 0)),
            pl.BlockSpec((2, 1, days, width_y), lambda i: (0, jnp.maximum(i * group - 1, 0), 0, 0)),
            pl.BlockSpec(
                (2, 1, days, width_y),
                lambda i: (0, jnp.minimum(i * group + group, width_x - 1), 0, 0),
            ),
            side_spec, side_spec, rim_spec, rim_spec, rim_spec, metric_spec, metric_spec,
        ],
        out_specs=[
            pl.BlockSpec((2 * days, group * width_y), lambda i: (0, i)),
            pl.BlockSpec((blocks, size, size), lambda i: (0, 0, 0)),
        ],
        out_shape=[
            jax.ShapeDtypeStruct((2 * days, width_x * width_y), BF16),
            jax.ShapeDtypeStruct((blocks, size, size), F32),
        ],
        scratch_shapes=[pltpu.VMEM((2 * days, 2 * days), F32)],
        compiler_params=pltpu.CompilerParams(vmem_limit_bytes=48 * MB),
        name="stencil_gram",
    )(moved, moved, moved, west, east, south, north, fold, lon, lat)


def all_sum(x):
    moves = []
    for axis in ("lat", "lon"):
        count = lax.axis_size(axis)
        assert count & (count - 1) == 0
        for bit in range(count.bit_length() - 1):
            moves.append((axis, bit))
    shape = x.shape
    x = x.reshape(-1, shape[-1])
    taken = []

    def swap(block, axis, bit):
        return lax.ppermute(
            block, axis, [(i, i ^ 1 << bit) for i in range(lax.axis_size(axis))]
        )

    for axis, bit in moves:
        halve = x.shape[0] % 16 == 0
        if halve:
            half = x.shape[0] // 2
            high = (lax.axis_index(axis) >> bit) & 1
            keep = lax.dynamic_slice_in_dim(x, high * half, half, 0)
            send = lax.dynamic_slice_in_dim(x, (1 - high) * half, half, 0)
            x = keep + swap(send, axis, bit)
        else:
            x = x + swap(x, axis, bit)
        taken.append(halve)
    for (axis, bit), halve in reversed(list(zip(moves, taken))):
        if halve:
            high = (lax.axis_index(axis) >> bit) & 1
            other = swap(x, axis, bit)
            x = jnp.where(
                high == 1, jnp.concatenate([other, x], 0), jnp.concatenate([x, other], 0)
            )
    return x.reshape(shape)


def pick_kernel(index_ref, fields_ref, out_ref, rows, picked):
    step = pl.program_id(0)
    columns, cells = fields_ref.shape
    count = out_ref.shape[0]
    parts = columns // 128

    @pl.when(step == 0)
    def _():
        unit = jnp.where(iota((128, 128), 0) == iota((128, 128), 1), 1.0, 0.0).astype(BF16)

        def turn(i, _):
            at = pl.multiple_of(i * 128, 128)
            block = fields_ref[:, pl.ds(at, 128)]
            turned = lax.dot_general(unit, block, NT, preferred_element_type=F32)
            for c in range(parts):
                rows[pl.ds(at * parts + c, 128, stride=parts), :] = turned[:, c * 128 : (c + 1) * 128]
            return 0

        lax.fori_loop(0, cells // 128, turn, 0)

    unroll = 16

    def move(i, _):
        for j in range(unroll):
            r = i * unroll + j
            source = pl.multiple_of(index_ref[step * count + r] * parts, parts)
            target = pl.multiple_of(r * parts, parts)
            picked[pl.ds(target, parts), :] = rows[pl.ds(source, parts), :]
        return 0

    lax.fori_loop(0, count // unroll, move, 0)
    for c in range(parts):
        out_ref[:, c * 128 : (c + 1) * 128] = picked[pl.ds(c, count, stride=parts), :].astype(BF16)


def pick(wet_index, fields):
    columns, cells = fields.shape
    count = next(c for c in (768, 512, 256, 128, cells) if cells % c == 0)
    parts = columns // 128
    return pl.pallas_call(
        pick_kernel,
        grid_spec=pltpu.PrefetchScalarGridSpec(
            num_scalar_prefetch=1,
            grid=(cells // count,),
            in_specs=[pl.BlockSpec((columns, cells), lambda i, _: (0, 0))],
            out_specs=pl.BlockSpec((count, columns), lambda i, _: (i, 0)),
            scratch_shapes=[
                pltpu.VMEM((cells * parts, 128), F32),
                pltpu.VMEM((count * parts, 128), F32),
            ],
        ),
        out_shape=jax.ShapeDtypeStruct((cells, columns), BF16),
        compiler_params=pltpu.CompilerParams(vmem_limit_bytes=48 * MB),
        name="pick",
    )(wet_index, fields)


def product_kernel(high_ref, low_ref, rows_ref, out_ref):
    columns = rows_ref.shape[1]
    half = columns // 2

    def dot(w, s):
        return lax.dot_general(w, s, NT, preferred_element_type=F32)

    s = rows_ref[:, :half]
    top = dot(low_ref[:half, :half], s) + dot(high_ref[:half, :half], s)
    out_ref[:half, :] = top.astype(BF16)
    s = rows_ref[...]
    bottom = dot(low_ref[half:, :], s) + dot(high_ref[half:, :], s)
    out_ref[half:, :] = bottom.astype(BF16)


def product(high, low, rows):
    cells, columns = rows.shape
    width = next(c for c in (1024, 512, 256, 128, cells) if cells % c == 0)
    factor_spec = pl.BlockSpec((columns, columns), lambda i: (0, 0))
    return pl.pallas_call(
        product_kernel,
        grid=(cells // width,),
        in_specs=[factor_spec, factor_spec, pl.BlockSpec((width, columns), lambda i: (i, 0))],
        out_specs=pl.BlockSpec((columns, width), lambda i: (0, i)),
        out_shape=jax.ShapeDtypeStruct((columns, cells), BF16),
        compiler_params=pltpu.CompilerParams(vmem_limit_bytes=48 * MB),
        name="product",
    )(high, low, rows)


def sublane(x, t):
    return jnp.broadcast_to(x[t : t + 1, :], x.shape)


def inverse_factor(block):
    size = block.shape[0]
    count = size // 8
    lane = iota((8, size), 1)
    row = iota((8, size), 0)
    tiles = [block[8 * p : 8 * p + 8, :] for p in range(count)]
    out = []
    for p in range(count):
        base = 8 * p
        cols = {
            q: [jnp.broadcast_to(tiles[q][:, base + t : base + t + 1], (8, size)) for t in range(8)]
            for q in range(p, count)
        }
        own = (lane >= base) & (lane < base + 8)
        work = jnp.where(own, jnp.where(lane == base + row, 1.0, 0.0), tiles[p])
        head = cols[p]
        done = jnp.zeros((8, size), F32)
        pivots = jnp.ones((8, size), F32)
        for t in range(8):
            at = row == t
            pivot = sublane(head[t], t)
            inverse = 1.0 / pivot
            coef = jnp.where(at, inverse, -head[t] * inverse)
            line = sublane(work, t)
            done = jnp.where(at, line, done)
            pivots = jnp.where(at, pivot, pivots)
            for u in range(t + 1, 8):
                head[u] = jnp.where(at, 0.0, head[u]) + coef * sublane(head[u], t)
            work = jnp.where(at, 0.0, work) + coef * line
        out.append(jnp.where(lane <= base + row, done * lax.rsqrt(pivots), 0.0))
        lines = [sublane(work, t) for t in range(8)]
        for q in range(p + 1, count):
            terms = [cols[q][t] * lines[t] for t in range(8)]
            while len(terms) > 1:
                terms = [terms[i] + terms[i + 1] for i in range(0, len(terms), 2)]
            tiles[q] = jnp.where(own, 0.0, tiles[q]) - terms[0]
    return jnp.concatenate(out, axis=0)


def factor_kernel(scale, pieces_ref, r_ref, high_ref, low_ref, work):
    columns = r_ref.shape[0]
    size = pieces_ref.shape[1]
    count = columns // size
    at = 0
    for i in range(count):
        for j in range(i, count):
            work[i * size : (i + 1) * size, j * size : (j + 1) * size] = pieces_ref[at]
            at += 1
        if i:
            work[i * size : (i + 1) * size, : i * size] = jnp.zeros((size, i * size), F32)

    def dot(a, b, dims):
        return lax.dot_general(
            a, b, dims, preferred_element_type=F32, precision=lax.Precision.HIGHEST
        )

    lane = iota((size, columns), 1)

    def step(k, _):
        here = pl.multiple_of(k * size, size)
        diagonal = work[pl.ds(here, size), pl.ds(here, size)]
        inverse = inverse_factor(diagonal)
        corner = dot(inverse, diagonal, NN)
        work[pl.ds(here, size), pl.ds(here, size)] = jnp.where(
            iota((size, size), 0) == iota((size, size), 1), 1.0, 0.0
        )
        fresh = dot(inverse, work[pl.ds(here, size), :], NN)
        work[pl.ds(here, size), :] = fresh
        for i in range(1, count):

            @pl.when(i > k)
            def _():
                mine = slice(i * size, (i + 1) * size)
                work[mine, pl.ds(here, size)] = jnp.zeros((size, size), F32)
                work[mine, :] -= dot(work[pl.ds(here, size), mine], work[pl.ds(here, size), :], TN)

        known = jnp.where(lane < here + size, fresh * scale, 0.0)
        high = known.astype(BF16)
        high_ref[pl.ds(here, size), :] = high
        low_ref[pl.ds(here, size), :] = (known - high.astype(F32)).astype(BF16)
        r_ref[pl.ds(here, size), :] = jnp.where(lane >= here + size, fresh * (1.0 / scale), 0.0)
        upper = iota((size, size), 0) <= iota((size, size), 1)
        r_ref[pl.ds(here, size), pl.ds(here, size)] = jnp.where(upper, corner * (1.0 / scale), 0.0)
        return 0

    lax.fori_loop(0, count, step, 0)


def factor(pieces, columns, scale):
    vmem = pl.BlockSpec(memory_space=pltpu.VMEM)
    square = (columns, columns)
    return pl.pallas_call(
        functools.partial(factor_kernel, scale),
        in_specs=[vmem],
        out_specs=[vmem, vmem, vmem],
        out_shape=[
            jax.ShapeDtypeStruct(square, F32),
            jax.ShapeDtypeStruct(square, BF16),
            jax.ShapeDtypeStruct(square, BF16),
        ],
        scratch_shapes=[pltpu.VMEM(square, F32)],
        compiler_params=pltpu.CompilerParams(vmem_limit_bytes=40 * MB),
        name="factor",
    )(pieces)


def shards(velocity, lon_metric, lat_metric, wet_index, wet_count):
    days = velocity.shape[1]
    cells = velocity.shape[2] * velocity.shape[3]
    columns = 2 * days
    lats, lons = lax.axis_size("lat"), lax.axis_size("lon")
    moved, south, north, fold = relayout(velocity)
    east_route = [(i, (i + 1) % lons) for i in range(lons)]
    west = lax.ppermute(moved[:, -1], "lon", east_route)
    east = lax.ppermute(moved[:, 0], "lon", [(t, s) for s, t in east_route])
    up = [(i, i + 1) for i in range(lats - 1)]
    below = lax.ppermute(north, "lat", up)
    above = lax.ppermute(south, "lat", [(t, s) for s, t in up])
    top = (lats - 1) * lons
    mirrored = lax.ppermute(fold, ("lat", "lon"), [(top + i, top + lons - 1 - i) for i in range(lons)])
    lon, lat = wet_metrics(wet_index, wet_count, lon_metric, lat_metric)
    size = min(128, columns)
    fields, gram = stencil(moved, west, east, below, above, mirrored, lon, lat, size)
    rows = pick(wet_index, fields)
    scale = math.sqrt(cells * lats * lons)
    triangle, high, low = factor(all_sum(gram), columns, scale)
    return product(high, low, rows), triangle


def solution(mesh):
    placed = (
        P(None, None, "lon", "lat"),
        P("lon", "lat"),
        P("lon", "lat"),
        P(("lat", "lon")),
        P(("lat", "lon")),
    )
    return jax.shard_map(
        shards,
        mesh=mesh,
        in_specs=placed,
        out_specs=(P(None, ("lat", "lon")), P()),
        check_vma=False,
    )
```

```python
import functools
import math

import jax
import jax.numpy as jnp
from jax import lax
from jax.experimental import pallas as pl
from jax.experimental.pallas import tpu as pltpu
from jax.sharding import PartitionSpec as P

F32 = jnp.float32
BF16 = jnp.bfloat16
MB = 1 << 20
ROOM = 24 * MB
TOKEN = jax.ShapeDtypeStruct((8, 128), F32)
NN = (((1,), (0,)), ((), ()))
NT = (((1,), (1,)), ((), ()))
TN = (((0,), (0,)), ((), ()))


def iota(shape, dim):
    return lax.broadcasted_iota(jnp.int32, shape, dim)


def lat_difference(width_y):
    wide = 2 * width_y
    k = iota((wide, wide), 0)
    n = iota((wide, wide), 1)
    same = k // width_y == n // width_y
    diff = jnp.where(same & (k == n + 1), 1.0, 0.0) - jnp.where(same & (k == n - 1), 1.0, 0.0)
    return diff.astype(BF16)


def gram_of(block, days):
    upper = lax.dot_general(block[:days, :], block, NT, preferred_element_type=F32)
    lower = lax.dot_general(block[days:, :], block[days:, :], NT, preferred_element_type=F32)
    return upper, lower


def front_kernel(
    v_hbm, index_hbm, count_ref, lon_hbm, lat_hbm,
    fields_hbm, total, lon_out, lat_out, south_ref, second_ref, north_ref, before_ref, fold_ref,
    x0_ref, x1_ref, x2_ref, x3_ref,
    index_ref, lon_ref, lat_ref, raw, moved, stage, lon_in, lat_in, sems, out_sems, small_sems,
):
    fields, days, width_x, width_y = v_hbm.shape
    step = raw.shape[2]
    half = width_y // 2

    def fetch(i):
        return pltpu.make_async_copy(
            v_hbm.at[:, pl.ds(i * step, step)], raw.at[i], sems.at[i]
        )

    small = [
        pltpu.make_async_copy(source, target, small_sems.at[i])
        for i, (source, target) in enumerate(
            ((index_hbm, index_ref), (lon_hbm, lon_ref), (lat_hbm, lat_ref))
        )
    ]
    for copy in small:
        copy.start()
    for i in range(days // step):
        fetch(i).start()
    for copy in small:
        copy.wait()

    cells = index_ref.shape[1]
    index = index_ref[...]
    wet = iota(index.shape, 1) < count_ref[0]
    row = jnp.where(wet, index // width_y, -1)
    col = index % width_y
    pick_x = jnp.where(iota((width_x, cells), 0) == row, 1.0, 0.0).astype(BF16)
    pick_y = jnp.where(iota((width_y, cells), 0) == col, 1.0, 0.0).astype(BF16)
    mask = lax.dot_general(pick_x, pick_y, NT, preferred_element_type=F32)
    x = iota((width_x, width_y), 0)
    y = iota((width_x, width_y), 1)
    inner = (x > 0) & (x < width_x - 1) & (y > 0) & (y < width_y - 1)
    lon = 0.5 * lon_ref[...] * mask
    lat = 0.5 * lat_ref[...] * mask
    lon_out[...] = lon
    lat_out[...] = lat
    lon_in[...] = jnp.where(inner, lon, 0.0)
    lat_in[...] = jnp.where(inner, lat, 0.0)

    lane = iota((16, width_y), 1)

    def turn(i, _):
        fetch(i).wait()
        for d in range(0, step, 16):
            south = second = north = before = jnp.zeros((16, width_y), BF16)
            rows = pl.ds(pl.multiple_of(i * step + d, 16), 16)
            for f in range(fields):
                columns = jnp.swapaxes(raw[i, f, d : d + 16], 0, 1)
                moved[f, :, rows, :] = columns
                for x in range(width_x):
                    at = f * half + x
                    turned = pltpu.roll(columns[x], at + 1, 1)
                    before = jnp.where(lane == (at - 1) % width_y, turned, before)
                    north = jnp.where(lane == at, turned, north)
                    south = jnp.where(lane == at + 1, turned, south)
                    second = jnp.where(lane == at + 2, turned, second)
            south_ref[rows, :] = pltpu.roll(south, width_y - 1, 1)
            second_ref[rows, :] = pltpu.roll(second, width_y - 2, 1)
            north_ref[rows, :] = north
            before_ref[rows, :] = pltpu.roll(before, 1, 1)
        return 0

    lax.fori_loop(0, days // step, turn, 0)
    k = iota((width_y, width_y), 0)
    n = iota((width_y, width_y), 1)
    mirror = (k // half == n // half) & (k + n == 2 * half * (n // half) + width_x - 1)
    mirror = jnp.where(mirror, -1.0, 0.0).astype(BF16)
    fold = lax.dot_general(north_ref[...], mirror, NN, preferred_element_type=F32)
    fold_ref[...] = fold.astype(BF16)
    x0_ref[...] = moved[:, 0]
    x1_ref[...] = moved[:, 1]
    x2_ref[...] = moved[:, width_x - 2]
    x3_ref[...] = moved[:, width_x - 1]

    wide = stage.shape[2]
    group = wide // width_y
    steps = width_x // group
    diff = lat_difference(width_y)
    total[...] = jnp.zeros_like(total)

    def send(i):
        slot = lax.rem(i, 2)
        place = pl.ds(pl.multiple_of(i * wide, wide), wide)
        return pltpu.make_async_copy(stage.at[slot], fields_hbm.at[:, place], out_sems.at[slot])

    def compute(i, _):
        slot = lax.rem(i, 2)

        @pl.when(i >= 2)
        def _():
            send(i - 2).wait()

        for g in range(group):
            x = i * group + g
            east = jnp.minimum(x + 1, width_x - 1)
            west = jnp.maximum(x - 1, 0)
            here = jnp.concatenate([moved[0, x], moved[1, x]], axis=1)
            along = lax.dot_general(here, diff, NN, preferred_element_type=F32)
            lon = lon_in[pl.ds(x, 1), :]
            lat = lat_in[pl.ds(x, 1), :]
            across_u = moved[0, east].astype(F32) - moved[0, west].astype(F32)
            across_v = moved[1, east].astype(F32) - moved[1, west].astype(F32)
            zeta = lon * across_v - lat * along[:, :width_y]
            divergence = lon * across_u + lat * along[:, width_y:]
            place = slice(g * width_y, (g + 1) * width_y)
            stage[slot, :days, place] = zeta.astype(BF16)
            stage[slot, days:, place] = divergence.astype(BF16)
        send(i).start()
        upper, lower = gram_of(stage[slot], days)
        total[:days, :] += upper
        total[days:, days:] += lower
        return 0

    lax.fori_loop(0, steps, compute, 0)
    for i in range(max(steps - 2, 0), steps):
        send(i).wait()


def front(velocity, wet_index, wet_count, lon_metric, lat_metric):
    fields, days, width_x, width_y = velocity.shape
    assert width_x <= width_y // 2 - 2
    step = next(n for n in (32, 16) if days % n == 0)
    group = next(n for n in (8, 6, 4, 3, 2, 1) if width_x % n == 0)
    vmem = pl.BlockSpec(memory_space=pltpu.VMEM)
    hbm = pl.BlockSpec(memory_space=pl.ANY)
    metric = jax.ShapeDtypeStruct((width_x, width_y), F32)
    edge = jax.ShapeDtypeStruct((days, width_y), BF16)
    column = jax.ShapeDtypeStruct((fields, days, width_y), BF16)
    return pl.pallas_call(
        front_kernel,
        in_specs=[hbm, hbm, pl.BlockSpec(memory_space=pltpu.SMEM), hbm, hbm],
        out_specs=[hbm] + [vmem] * 12,
        out_shape=[
            jax.ShapeDtypeStruct((2 * days, width_x * width_y), BF16),
            jax.ShapeDtypeStruct((2 * days, 2 * days), F32),
            metric, metric, edge, edge, edge, edge, edge, column, column, column, column,
        ],
        scratch_shapes=[
            pltpu.VMEM((1, width_x * width_y), jnp.int32),
            pltpu.VMEM((width_x, width_y), F32),
            pltpu.VMEM((width_x, width_y), F32),
            pltpu.VMEM((days // step, fields, step, width_x, width_y), BF16),
            pltpu.VMEM((fields, width_x, days, width_y), BF16),
            pltpu.VMEM((2, 2 * days, group * width_y), BF16),
            pltpu.VMEM((width_x, width_y), F32),
            pltpu.VMEM((width_x, width_y), F32),
            pltpu.SemaphoreType.DMA((days // step,)),
            pltpu.SemaphoreType.DMA((2,)),
            pltpu.SemaphoreType.DMA((3,)),
        ],
        compiler_params=pltpu.CompilerParams(vmem_limit_bytes=50 * MB),
        name="front",
    )(velocity, wet_index.reshape(1, -1), wet_count, lon_metric, lat_metric)


def rim_kernel(
    x0_ref, x1_ref, x2_ref, x3_ref, west_ref, east_ref, below_ref, above_ref, mirrored_ref,
    south_ref, second_ref, north_ref, before_ref, lon_ref, lat_ref, total_ref,
    gram_ref, rows_ref, ends_ref,
):
    _, days, width_y = x0_ref.shape
    width_x = lon_ref.shape[0]
    half = width_y // 2
    below = below_ref[...].astype(F32)
    above = above_ref[...].astype(F32) + mirrored_ref[...].astype(F32)
    lane = iota((1, width_y), 1)

    diff = lat_difference(width_y)
    column_lane = iota((days, width_y), 1)
    for end, x, own_ref, west, east in (
        (0, 0, x0_ref, west_ref, x1_ref),
        (1, width_x - 1, x3_ref, x2_ref, east_ref),
    ):
        here = jnp.concatenate([own_ref[0], own_ref[1]], axis=1)
        along = lax.dot_general(here, diff, NN, preferred_element_type=F32)
        lon = lon_ref[x : x + 1, :]
        lat = lat_ref[x : x + 1, :]
        flow = []
        for f in range(2):
            own = along[:, f * width_y : (f + 1) * width_y]
            at = f * half + x
            own = own - jnp.where(column_lane == 0, below[:, at : at + 1], 0.0)
            own = own + jnp.where(column_lane == width_y - 1, above[:, at : at + 1], 0.0)
            flow.append(own)
        across_u = east[0].astype(F32) - west[0].astype(F32)
        across_v = east[1].astype(F32) - west[1].astype(F32)
        ends_ref[end, :days, :] = (lon * across_v - lat * flow[0]).astype(BF16)
        ends_ref[end, days:, :] = (lon * across_u + lat * flow[1]).astype(BF16)

    fill = jnp.zeros((width_y - width_x, width_y), F32)
    lon_turned = jnp.concatenate([lon_ref[...], fill], axis=0).T
    lat_turned = jnp.concatenate([lat_ref[...], fill], axis=0).T
    spot = lane % half
    between = (spot > 0) & (spot < width_x - 1)
    parts = []
    for y, row, low, high in (
        (0, south_ref, below, second_ref[...].astype(F32)),
        (width_y - 1, north_ref, before_ref[...].astype(F32), above),
    ):
        lon = lon_turned[y : y + 1, :]
        lat = lat_turned[y : y + 1, :]
        lon = jnp.where(between, jnp.where(lane < half, lon, pltpu.roll(lon, half, 1)), 0.0)
        lat = jnp.where(between, jnp.where(lane < half, -lat, pltpu.roll(lat, half, 1)), 0.0)
        own = row[...].astype(F32)
        across = pltpu.roll(own, width_y - 1, 1) - pltpu.roll(own, 1, 1)
        parts.append(lon * pltpu.roll(across, half, 1) + lat * (high - low))
    low_lane = column_lane < half
    rows_ref[:days, :] = jnp.where(low_lane, parts[0], pltpu.roll(parts[1], half, 1)).astype(BF16)
    rows_ref[days:, :] = jnp.where(low_lane, pltpu.roll(parts[0], half, 1), parts[1]).astype(BF16)

    rim = jnp.concatenate([ends_ref[0], ends_ref[1], rows_ref[...]], axis=1)
    upper, lower = gram_of(rim, days)
    size = gram_ref.shape[1]
    at = 0
    for i in range(2 * days // size):
        for j in range(i, 2 * days // size):
            left = slice(i * size, (i + 1) * size)
            right = slice(j * size, (j + 1) * size)
            if i * size < days:
                extra = upper[left, right]
            else:
                extra = lower[
                    i * size - days : (i + 1) * size - days, j * size - days : (j + 1) * size - days
                ]
            gram_ref[at] = total_ref[left, right] + extra
            at += 1


def rim(ends, sides, edges, lon, lat, total, size):
    _, days, width_y = ends[0].shape
    count = 2 * days // size
    vmem = pl.BlockSpec(memory_space=pltpu.VMEM)
    operands = (*ends, *sides, *edges, lon, lat, total)
    return pl.pallas_call(
        rim_kernel,
        in_specs=[vmem] * len(operands),
        out_specs=[vmem] * 3,
        out_shape=[
            jax.ShapeDtypeStruct((count * (count + 1) // 2, size, size), F32),
            jax.ShapeDtypeStruct((2 * days, width_y), BF16),
            jax.ShapeDtypeStruct((2, 2 * days, width_y), BF16),
        ],
        compiler_params=pltpu.CompilerParams(vmem_limit_bytes=ROOM),
        name="rim",
    )(*operands)


def all_sum(x, beside):
    moves = []
    for axis in ("lat", "lon"):
        count = lax.axis_size(axis)
        assert count & (count - 1) == 0
        for bit in range(count.bit_length() - 1):
            moves.append((axis, bit))
    shape = x.shape
    x = x.reshape(-1, shape[-1])
    taken = []

    hops = 0

    def swap(block, axis, bit):
        nonlocal hops
        other = lax.ppermute(
            block, axis, [(i, i ^ 1 << bit) for i in range(lax.axis_size(axis))]
        )
        if hops in beside:
            other = other + beside[hops](block)[0, 0]
        hops += 1
        return other

    for axis, bit in moves:
        halve = x.shape[0] % 16 == 0 and x.shape[0] > shape[0] * 16
        if halve:
            half = x.shape[0] // 2
            high = (lax.axis_index(axis) >> bit) & 1
            keep = lax.dynamic_slice_in_dim(x, high * half, half, 0)
            send = lax.dynamic_slice_in_dim(x, (1 - high) * half, half, 0)
            x = keep + swap(send, axis, bit)
        else:
            x = x + swap(x, axis, bit)
        taken.append(halve)
    for (axis, bit), halve in reversed(list(zip(moves, taken))):
        if halve:
            high = (lax.axis_index(axis) >> bit) & 1
            other = swap(x, axis, bit)
            x = jnp.where(
                high == 1, jnp.concatenate([other, x], 0), jnp.concatenate([x, other], 0)
            )
    return x.reshape(shape)


def pick_kernel(
    piece, index_hbm, fields_hbm, rim_ref, ends_ref, after_ref, out_hbm, token_ref,
    index_ref, stage, rows, picked, turned_out, sems, out_sems,
):
    token_ref[...] = jnp.zeros_like(token_ref)
    columns, wide = rim_ref.shape
    count = out_hbm.shape[0]
    cells = fields_hbm.shape[1]
    width_x = cells // wide
    parts = columns // 128
    chunk = stage.shape[2]

    def fetch(i):
        return pltpu.make_async_copy(
            fields_hbm.at[:, i * chunk : (i + 1) * chunk], stage.at[i], sems.at[i]
        )

    places = pltpu.make_async_copy(index_hbm, index_ref, out_sems.at[2])
    places.start()
    for i in range(cells // chunk):
        fetch(i).start()
    unit = jnp.where(iota((wide, wide), 0) == iota((wide, wide), 1), 1.0, 0.0).astype(BF16)

    def turned(block):
        return lax.dot_general(unit, block, NT, preferred_element_type=F32)

    rim = turned(rim_ref[...])
    for i in range(cells // chunk):
        fetch(i).wait()
        for x in range(i * chunk // wide, (i + 1) * chunk // wide):
            at = x * wide * parts
            last = x == width_x - 1
            inside = x > 0 and not last
            if inside:
                start = x * wide - i * chunk
                block = turned(stage[i, :, start : start + wide])
            else:
                block = turned(ends_ref[int(last)])
            for c in range(parts):
                own = slice(c * 128, (c + 1) * 128)
                rows[pl.ds(at + c, wide, stride=parts), :] = block[:, own]
                if inside:
                    rows[at + c : at + c + 1, :] = rim[x : x + 1, own]
                    end = at + (wide - 1) * parts + c
                    rows[end : end + 1, :] = rim[wide // 2 + x : wide // 2 + x + 1, own]

    places.wait()
    share = picked.shape[1] // parts
    block = turned_out.shape[1]

    def row(at):
        return rows[pl.ds(pl.multiple_of(index_ref[at], parts), parts), :]

    def send(i):
        return pltpu.make_async_copy(
            turned_out.at[i % 2], out_hbm.at[i * block : (i + 1) * block], out_sems.at[i % 2]
        )

    for i in range(count // block):
        if i >= 2:
            send(i - 2).wait()

        def body(k, _):
            start = k * share
            slot = lax.rem(k, 2)
            source = piece * count + i * block + start
            for j in range(0, share, 2):
                pair = jnp.concatenate([row(source + j), row(source + j + 1)], axis=0)
                picked[slot, j * parts : (j + 2) * parts, :] = pair
            for c in range(parts):
                part = picked[slot, pl.ds(c, share, stride=parts), :]
                turned_out[
                    i % 2, pl.ds(pl.multiple_of(start, share), share), c * 128 : (c + 1) * 128
                ] = part.astype(BF16)
            return 0

        lax.fori_loop(0, block // share, body, 0)
        send(i).start()
    for i in range(max(count // block - 2, 0), count // block):
        send(i).wait()


def pick(piece, pieces, places, fields, rim, ends, after):
    columns, cells = fields.shape
    wide = rim.shape[1]
    parts = columns // 128
    share = 64
    block = next(n for n in (768, 512, 256, 128, 64) if cells % (pieces * n) == 0)
    chunk = next(n * wide for n in (8, 6, 4, 3, 2, 1) if cells % (n * wide) == 0)
    vmem = pl.BlockSpec(memory_space=pltpu.VMEM)
    hbm = pl.BlockSpec(memory_space=pl.ANY)
    return pl.pallas_call(
        functools.partial(pick_kernel, piece),
        in_specs=[hbm, hbm, vmem, vmem, hbm],
        out_specs=[hbm, vmem],
        out_shape=[jax.ShapeDtypeStruct((cells // pieces, columns), BF16), TOKEN],
        scratch_shapes=[
            pltpu.SMEM((cells,), jnp.int32),
            pltpu.VMEM((cells // chunk, columns, chunk), BF16),
            pltpu.VMEM((cells * parts, 128), F32),
            pltpu.VMEM((2, share * parts, 128), F32),
            pltpu.VMEM((2, block, columns), BF16),
            pltpu.SemaphoreType.DMA((cells // chunk,)),
            pltpu.SemaphoreType.DMA((3,)),
        ],
        compiler_params=pltpu.CompilerParams(vmem_limit_bytes=50 * MB),
        name="pick",
    )(places, fields, rim, ends, after)


def product_kernel(steps, high_ref, low_ref, *refs):
    out_ref = refs[-1]
    columns = high_ref.shape[0]
    half = columns // 2

    def dot(w, s):
        return lax.dot_general(w, s, NT, preferred_element_type=F32)

    for piece, rows_ref in enumerate(refs[:-1]):

        @pl.when(pl.program_id(0) // steps == piece)
        def _():
            s = rows_ref[...]
            low = s[:, :half]
            top = dot(low_ref[:half, :half], low) + dot(high_ref[:half, :half], low)
            out_ref[:half, :] = top.astype(BF16)
            bottom = dot(low_ref[half:, :], s) + dot(high_ref[half:, :], s)
            out_ref[half:, :] = bottom.astype(BF16)


def product(high, low, pieces):
    count, columns = pieces[0].shape
    width = next(c for c in (768, 512, 256, 128) if count % c == 0)
    steps = count // width
    vmem = pl.BlockSpec(memory_space=pltpu.VMEM)
    return pl.pallas_call(
        functools.partial(product_kernel, steps),
        grid=(len(pieces) * steps,),
        in_specs=[vmem, vmem]
        + [
            pl.BlockSpec((width, columns), lambda i, k=k: (jnp.clip(i - k * steps, 0, steps - 1), 0))
            for k in range(len(pieces))
        ],
        out_specs=pl.BlockSpec((columns, width), lambda i: (0, i)),
        out_shape=jax.ShapeDtypeStruct((columns, len(pieces) * count), BF16),
        compiler_params=pltpu.CompilerParams(vmem_limit_bytes=50 * MB),
        name="product",
    )(high, low, *pieces)


def sublane(x, t):
    return jnp.broadcast_to(x[t : t + 1, :], x.shape)


def inverse_factor(block):
    size = block.shape[0]
    count = size // 8
    lane = iota((8, size), 1)
    row = iota((8, size), 0)
    tiles = [block[8 * p : 8 * p + 8, :] for p in range(count)]
    out = []
    for p in range(count):
        base = 8 * p
        cols = {
            q: [jnp.broadcast_to(tiles[q][:, base + t : base + t + 1], (8, size)) for t in range(8)]
            for q in range(p, count)
        }
        own = (lane >= base) & (lane < base + 8)
        work = jnp.where(own, jnp.where(lane == base + row, 1.0, 0.0), tiles[p])
        head = cols[p]
        done = jnp.zeros((8, size), F32)
        pivots = jnp.ones((8, size), F32)
        for t in range(8):
            at = row == t
            pivot = sublane(head[t], t)
            inverse = 1.0 / pivot
            coef = jnp.where(at, inverse, -head[t] * inverse)
            line = sublane(work, t)
            done = jnp.where(at, line, done)
            pivots = jnp.where(at, pivot, pivots)
            for u in range(t + 1, 8):
                head[u] = jnp.where(at, 0.0, head[u]) + coef * sublane(head[u], t)
            work = jnp.where(at, 0.0, work) + coef * line
        out.append(jnp.where(lane <= base + row, done * lax.rsqrt(pivots), 0.0))
        lines = [sublane(work, t) for t in range(8)]
        for q in range(p + 1, count):
            terms = [cols[q][t] * lines[t] for t in range(8)]
            while len(terms) > 1:
                terms = [terms[i] + terms[i + 1] for i in range(0, len(terms), 2)]
            tiles[q] = jnp.where(own, 0.0, tiles[q]) - terms[0]
    return jnp.concatenate(out, axis=0)


def factor_kernel(scale, pieces_ref, r_ref, high_ref, low_ref, work):
    columns = r_ref.shape[0]
    size = pieces_ref.shape[1]
    count = columns // size
    at = 0
    for i in range(count):
        for j in range(i, count):
            work[i * size : (i + 1) * size, j * size : (j + 1) * size] = pieces_ref[at]
            at += 1
        if i:
            work[i * size : (i + 1) * size, : i * size] = jnp.zeros((size, i * size), F32)

    def dot(a, b, dims):
        return lax.dot_general(
            a, b, dims, preferred_element_type=F32, precision=lax.Precision.HIGHEST
        )

    lane = iota((size, columns), 1)

    def step(k, _):
        here = pl.multiple_of(k * size, size)
        diagonal = work[pl.ds(here, size), pl.ds(here, size)]
        inverse = inverse_factor(diagonal)
        corner = dot(inverse, diagonal, NN)
        work[pl.ds(here, size), pl.ds(here, size)] = jnp.where(
            iota((size, size), 0) == iota((size, size), 1), 1.0, 0.0
        )
        fresh = dot(inverse, work[pl.ds(here, size), :], NN)
        work[pl.ds(here, size), :] = fresh
        for i in range(1, count):

            @pl.when(i > k)
            def _():
                mine = slice(i * size, (i + 1) * size)
                work[mine, pl.ds(here, size)] = jnp.zeros((size, size), F32)
                work[mine, :] -= dot(work[pl.ds(here, size), mine], work[pl.ds(here, size), :], TN)

        known = jnp.where(lane < here + size, fresh * scale, 0.0)
        high = known.astype(BF16)
        high_ref[pl.ds(here, size), :] = high
        low_ref[pl.ds(here, size), :] = (known - high.astype(F32)).astype(BF16)
        r_ref[pl.ds(here, size), :] = jnp.where(lane >= here + size, fresh * (1.0 / scale), 0.0)
        upper = iota((size, size), 0) <= iota((size, size), 1)
        r_ref[pl.ds(here, size), pl.ds(here, size)] = jnp.where(upper, corner * (1.0 / scale), 0.0)
        return 0

    lax.fori_loop(0, count, step, 0)


def factor(pieces, columns, scale):
    vmem = pl.BlockSpec(memory_space=pltpu.VMEM)
    square = (columns, columns)
    return pl.pallas_call(
        functools.partial(factor_kernel, scale),
        in_specs=[vmem],
        out_specs=[vmem] * 3,
        out_shape=[
            jax.ShapeDtypeStruct(square, F32),
            jax.ShapeDtypeStruct(square, BF16),
            jax.ShapeDtypeStruct(square, BF16),
        ],
        scratch_shapes=[pltpu.VMEM(square, F32)],
        compiler_params=pltpu.CompilerParams(vmem_limit_bytes=ROOM),
        name="factor",
    )(pieces)


def shards(velocity, lon_metric, lat_metric, wet_index, wet_count):
    days = velocity.shape[1]
    cells = velocity.shape[2] * velocity.shape[3]
    columns = 2 * days
    lats, lons = lax.axis_size("lat"), lax.axis_size("lon")
    fields, total, lon, lat, south, second, north, before, fold, *outer = front(
        velocity, wet_index, wet_count, lon_metric, lat_metric
    )
    east_route = [(i, (i + 1) % lons) for i in range(lons)]
    west = lax.ppermute(outer[3], "lon", east_route)
    east = lax.ppermute(outer[0], "lon", [(t, s) for s, t in east_route])
    up = [(i, i + 1) for i in range(lats - 1)]
    below = lax.ppermute(north, "lat", up)
    above = lax.ppermute(south, "lat", [(t, s) for s, t in up])
    top = (lats - 1) * lons
    mirrored = lax.ppermute(fold, ("lat", "lon"), [(top + i, top + lons - 1 - i) for i in range(lons)])
    sides = (west, east, below, above, mirrored)
    edges = (south, second, north, before)
    gram, rows, ends = rim(outer, sides, edges, lon, lat, total, min(128, columns))

    places = wet_index * (columns // 128)
    pieces = 1
    held = {}

    def picking(piece, after):
        held[piece], token = pick(piece, pieces, places, fields, rows, ends, after)
        return token

    beside = {2 + piece: functools.partial(picking, piece) for piece in range(pieces)}
    total = all_sum(gram, beside)
    scale = math.sqrt(cells * lats * lons)
    triangle, high, low = factor(total, columns, scale)
    return product(high, low, [held[piece] for piece in range(pieces)]), triangle


def solution(mesh):
    placed = (
        P(None, None, "lon", "lat"),
        P("lon", "lat"),
        P("lon", "lat"),
        P(("lat", "lon")),
        P(("lat", "lon")),
    )
    return jax.shard_map(
        shards,
        mesh=mesh,
        in_specs=placed,
        out_specs=(P(None, ("lat", "lon")), P()),
        check_vma=False,
    )
```

```python
import functools
import math

import jax
import jax.numpy as jnp
from jax import lax
from jax.experimental import pallas as pl
from jax.experimental.pallas import tpu as pltpu
from jax.sharding import PartitionSpec as P

F32 = jnp.float32
BF16 = jnp.bfloat16
MB = 1 << 20
ROOM = 24 * MB
TOKEN = jax.ShapeDtypeStruct((8, 128), F32)
NN = (((1,), (0,)), ((), ()))
NT = (((1,), (1,)), ((), ()))
TN = (((0,), (0,)), ((), ()))


def iota(shape, dim):
    return lax.broadcasted_iota(jnp.int32, shape, dim)


def lat_difference(width_y):
    wide = 2 * width_y
    k = iota((wide, wide), 0)
    n = iota((wide, wide), 1)
    same = k // width_y == n // width_y
    diff = jnp.where(same & (k == n + 1), 1.0, 0.0) - jnp.where(same & (k == n - 1), 1.0, 0.0)
    return diff.astype(BF16)


def gram_of(block, days):
    upper = lax.dot_general(block[:days, :], block, NT, preferred_element_type=F32)
    lower = lax.dot_general(block[days:, :], block[days:, :], NT, preferred_element_type=F32)
    return upper, lower


def front_kernel(
    v_hbm, cells_ref, count_ref,
    fields_hbm, total, lon_out, lat_out, south_ref, second_ref, north_ref, before_ref, fold_ref,
    x0_ref, x1_ref, x2_ref, x3_ref,
    raw, moved, stage, lon_in, lat_in, sems, out_sems,
):
    fields, days, width_x, width_y = v_hbm.shape
    step = raw.shape[2]
    half = width_y // 2

    def fetch(i):
        return pltpu.make_async_copy(
            v_hbm.at[:, pl.ds(i * step, step)], raw.at[i], sems.at[i]
        )

    for i in range(days // step):
        fetch(i).start()

    cells = width_x * width_y
    index = cells_ref[2].astype(jnp.int32)
    index = jnp.concatenate([index[x : x + 1, :] for x in range(width_x)], axis=1)
    wet = iota(index.shape, 1) < count_ref[0]
    row = jnp.where(wet, index // width_y, -1)
    col = index % width_y
    pick_x = jnp.where(iota((width_x, cells), 0) == row, 1.0, 0.0).astype(BF16)
    pick_y = jnp.where(iota((width_y, cells), 0) == col, 1.0, 0.0).astype(BF16)
    mask = lax.dot_general(pick_x, pick_y, NT, preferred_element_type=F32)
    at_x = iota((width_x, width_y), 0)
    at_y = iota((width_x, width_y), 1)
    inner = (at_x > 0) & (at_x < width_x - 1) & (at_y > 0) & (at_y < width_y - 1)
    lon = 0.5 * cells_ref[0] * mask
    lat = 0.5 * cells_ref[1] * mask
    lon_out[...] = lon
    lat_out[...] = lat
    lon_in[...] = jnp.where(inner, lon, 0.0)
    lat_in[...] = jnp.where(inner, lat, 0.0)

    lane = iota((16, width_y), 1)

    def turn(i, _):
        fetch(i).wait()
        for d in range(0, step, 16):
            south = second = north = before = jnp.zeros((16, width_y), BF16)
            rows = pl.ds(pl.multiple_of(i * step + d, 16), 16)
            for f in range(fields):
                columns = jnp.swapaxes(raw[i, f, d : d + 16], 0, 1)
                moved[f, :, rows, :] = columns
                for x in range(width_x):
                    at = f * half + x
                    turned = pltpu.roll(columns[x], at + 1, 1)
                    before = jnp.where(lane == (at - 1) % width_y, turned, before)
                    north = jnp.where(lane == at, turned, north)
                    south = jnp.where(lane == at + 1, turned, south)
                    second = jnp.where(lane == at + 2, turned, second)
            south_ref[rows, :] = pltpu.roll(south, width_y - 1, 1)
            second_ref[rows, :] = pltpu.roll(second, width_y - 2, 1)
            north_ref[rows, :] = north
            before_ref[rows, :] = pltpu.roll(before, 1, 1)
        return 0

    lax.fori_loop(0, days // step, turn, 0)
    k = iota((width_y, width_y), 0)
    n = iota((width_y, width_y), 1)
    mirror = (k // half == n // half) & (k + n == 2 * half * (n // half) + width_x - 1)
    mirror = jnp.where(mirror, -1.0, 0.0).astype(BF16)
    fold = lax.dot_general(north_ref[...], mirror, NN, preferred_element_type=F32)
    fold_ref[...] = fold.astype(BF16)
    x0_ref[...] = moved[:, 0]
    x1_ref[...] = moved[:, 1]
    x2_ref[...] = moved[:, width_x - 2]
    x3_ref[...] = moved[:, width_x - 1]

    wide = stage.shape[2]
    group = wide // width_y
    steps = width_x // group
    diff = lat_difference(width_y)
    total[...] = jnp.zeros_like(total)

    def send(i):
        slot = lax.rem(i, 2)
        place = pl.ds(pl.multiple_of(i * wide, wide), wide)
        return pltpu.make_async_copy(stage.at[slot], fields_hbm.at[:, place], out_sems.at[slot])

    def compute(i, _):
        slot = lax.rem(i, 2)

        @pl.when(i >= 2)
        def _():
            send(i - 2).wait()

        for g in range(group):
            x = i * group + g
            east = jnp.minimum(x + 1, width_x - 1)
            west = jnp.maximum(x - 1, 0)
            here = jnp.concatenate([moved[0, x], moved[1, x]], axis=1)
            along = lax.dot_general(here, diff, NN, preferred_element_type=F32)
            lon = lon_in[pl.ds(x, 1), :]
            lat = lat_in[pl.ds(x, 1), :]
            across_u = moved[0, east].astype(F32) - moved[0, west].astype(F32)
            across_v = moved[1, east].astype(F32) - moved[1, west].astype(F32)
            zeta = lon * across_v - lat * along[:, :width_y]
            divergence = lon * across_u + lat * along[:, width_y:]
            place = slice(g * width_y, (g + 1) * width_y)
            stage[slot, :days, place] = zeta.astype(BF16)
            stage[slot, days:, place] = divergence.astype(BF16)
        send(i).start()
        upper, lower = gram_of(stage[slot], days)
        total[:days, :] += upper
        total[days:, days:] += lower
        return 0

    lax.fori_loop(0, steps, compute, 0)
    for i in range(max(steps - 2, 0), steps):
        send(i).wait()


def front(velocity, wet_index, wet_count, lon_metric, lat_metric):
    fields, days, width_x, width_y = velocity.shape
    assert width_x <= width_y // 2 - 2
    step = next(n for n in (32, 16) if days % n == 0)
    places = wet_index.reshape(width_x, width_y).astype(F32)
    group = next(n for n in (8, 6, 4, 3, 2, 1) if width_x % n == 0)
    vmem = pl.BlockSpec(memory_space=pltpu.VMEM)
    hbm = pl.BlockSpec(memory_space=pl.ANY)
    metric = jax.ShapeDtypeStruct((width_x, width_y), F32)
    edge = jax.ShapeDtypeStruct((days, width_y), BF16)
    column = jax.ShapeDtypeStruct((fields, days, width_y), BF16)
    return pl.pallas_call(
        front_kernel,
        in_specs=[hbm, vmem, pl.BlockSpec(memory_space=pltpu.SMEM)],
        out_specs=[hbm] + [vmem] * 12,
        out_shape=[
            jax.ShapeDtypeStruct((2 * days, width_x * width_y), BF16),
            jax.ShapeDtypeStruct((2 * days, 2 * days), F32),
            metric, metric, edge, edge, edge, edge, edge, column, column, column, column,
        ],
        scratch_shapes=[
            pltpu.VMEM((days // step, fields, step, width_x, width_y), BF16),
            pltpu.VMEM((fields, width_x, days, width_y), BF16),
            pltpu.VMEM((2, 2 * days, group * width_y), BF16),
            pltpu.VMEM((width_x, width_y), F32),
            pltpu.VMEM((width_x, width_y), F32),
            pltpu.SemaphoreType.DMA((days // step,)),
            pltpu.SemaphoreType.DMA((2,)),
        ],
        compiler_params=pltpu.CompilerParams(vmem_limit_bytes=50 * MB),
        name="front",
    )(velocity, jnp.stack([lon_metric, lat_metric, places]), wet_count)


def rim_kernel(
    x0_ref, x1_ref, x2_ref, x3_ref, west_ref, east_ref, below_ref, above_ref, mirrored_ref,
    south_ref, second_ref, north_ref, before_ref, lon_ref, lat_ref, total_ref,
    gram_ref, rows_ref, ends_ref,
):
    _, days, width_y = x0_ref.shape
    width_x = lon_ref.shape[0]
    half = width_y // 2
    below = below_ref[...].astype(F32)
    above = above_ref[...].astype(F32) + mirrored_ref[...].astype(F32)
    lane = iota((1, width_y), 1)

    diff = lat_difference(width_y)
    column_lane = iota((days, width_y), 1)
    for end, x, own_ref, west, east in (
        (0, 0, x0_ref, west_ref, x1_ref),
        (1, width_x - 1, x3_ref, x2_ref, east_ref),
    ):
        here = jnp.concatenate([own_ref[0], own_ref[1]], axis=1)
        along = lax.dot_general(here, diff, NN, preferred_element_type=F32)
        lon = lon_ref[x : x + 1, :]
        lat = lat_ref[x : x + 1, :]
        flow = []
        for f in range(2):
            own = along[:, f * width_y : (f + 1) * width_y]
            at = f * half + x
            own = own - jnp.where(column_lane == 0, below[:, at : at + 1], 0.0)
            own = own + jnp.where(column_lane == width_y - 1, above[:, at : at + 1], 0.0)
            flow.append(own)
        across_u = east[0].astype(F32) - west[0].astype(F32)
        across_v = east[1].astype(F32) - west[1].astype(F32)
        ends_ref[end, :days, :] = (lon * across_v - lat * flow[0]).astype(BF16)
        ends_ref[end, days:, :] = (lon * across_u + lat * flow[1]).astype(BF16)

    fill = jnp.zeros((width_y - width_x, width_y), F32)
    lon_turned = jnp.concatenate([lon_ref[...], fill], axis=0).T
    lat_turned = jnp.concatenate([lat_ref[...], fill], axis=0).T
    spot = lane % half
    between = (spot > 0) & (spot < width_x - 1)
    parts = []
    for y, row, low, high in (
        (0, south_ref, below, second_ref[...].astype(F32)),
        (width_y - 1, north_ref, before_ref[...].astype(F32), above),
    ):
        lon = lon_turned[y : y + 1, :]
        lat = lat_turned[y : y + 1, :]
        lon = jnp.where(between, jnp.where(lane < half, lon, pltpu.roll(lon, half, 1)), 0.0)
        lat = jnp.where(between, jnp.where(lane < half, -lat, pltpu.roll(lat, half, 1)), 0.0)
        own = row[...].astype(F32)
        across = pltpu.roll(own, width_y - 1, 1) - pltpu.roll(own, 1, 1)
        parts.append(lon * pltpu.roll(across, half, 1) + lat * (high - low))
    low_lane = column_lane < half
    rows_ref[:days, :] = jnp.where(low_lane, parts[0], pltpu.roll(parts[1], half, 1)).astype(BF16)
    rows_ref[days:, :] = jnp.where(low_lane, pltpu.roll(parts[0], half, 1), parts[1]).astype(BF16)

    rim = jnp.concatenate([ends_ref[0], ends_ref[1], rows_ref[...]], axis=1)
    upper, lower = gram_of(rim, days)
    size = gram_ref.shape[1]
    at = 0
    for i in range(2 * days // size):
        for j in range(i, 2 * days // size):
            left = slice(i * size, (i + 1) * size)
            right = slice(j * size, (j + 1) * size)
            if i * size < days:
                extra = upper[left, right]
            else:
                extra = lower[
                    i * size - days : (i + 1) * size - days, j * size - days : (j + 1) * size - days
                ]
            gram_ref[at] = total_ref[left, right] + extra
            at += 1


def rim(ends, sides, edges, lon, lat, total, size):
    _, days, width_y = ends[0].shape
    count = 2 * days // size
    vmem = pl.BlockSpec(memory_space=pltpu.VMEM)
    operands = (*ends, *sides, *edges, lon, lat, total)
    return pl.pallas_call(
        rim_kernel,
        in_specs=[vmem] * len(operands),
        out_specs=[vmem] * 3,
        out_shape=[
            jax.ShapeDtypeStruct((count * (count + 1) // 2, size, size), F32),
            jax.ShapeDtypeStruct((2 * days, width_y), BF16),
            jax.ShapeDtypeStruct((2, 2 * days, width_y), BF16),
        ],
        compiler_params=pltpu.CompilerParams(vmem_limit_bytes=ROOM),
        name="rim",
    )(*operands)


def all_sum(x, beside):
    moves = []
    for axis in ("lat", "lon"):
        count = lax.axis_size(axis)
        assert count & (count - 1) == 0
        for bit in range(count.bit_length() - 1):
            moves.append((axis, bit))
    shape = x.shape
    x = x.reshape(-1, shape[-1])
    taken = []

    hops = 0

    def swap(block, axis, bit):
        nonlocal hops
        other = lax.ppermute(
            block, axis, [(i, i ^ 1 << bit) for i in range(lax.axis_size(axis))]
        )
        if hops in beside:
            other = other + beside[hops](block)[0, 0]
        hops += 1
        return other

    for axis, bit in moves:
        halve = x.shape[0] % 16 == 0 and x.shape[0] > shape[0] * 16
        if halve:
            half = x.shape[0] // 2
            high = (lax.axis_index(axis) >> bit) & 1
            keep = lax.dynamic_slice_in_dim(x, high * half, half, 0)
            send = lax.dynamic_slice_in_dim(x, (1 - high) * half, half, 0)
            x = keep + swap(send, axis, bit)
        else:
            x = x + swap(x, axis, bit)
        taken.append(halve)
    for (axis, bit), halve in reversed(list(zip(moves, taken))):
        if halve:
            high = (lax.axis_index(axis) >> bit) & 1
            other = swap(x, axis, bit)
            x = jnp.where(
                high == 1, jnp.concatenate([other, x], 0), jnp.concatenate([x, other], 0)
            )
    return x.reshape(shape)


def pick_kernel(
    piece, index_hbm, fields_hbm, rim_ref, ends_ref, after_ref, out_hbm, token_ref,
    index_ref, stage, rows, picked, turned_out, sems, out_sems,
):
    token_ref[...] = jnp.zeros_like(token_ref)
    columns, wide = rim_ref.shape
    count = out_hbm.shape[0]
    cells = fields_hbm.shape[1]
    width_x = cells // wide
    parts = columns // 128
    chunk = stage.shape[2]

    def fetch(i):
        return pltpu.make_async_copy(
            fields_hbm.at[:, i * chunk : (i + 1) * chunk], stage.at[i], sems.at[i]
        )

    places = pltpu.make_async_copy(index_hbm, index_ref, out_sems.at[2])
    places.start()
    for i in range(cells // chunk):
        fetch(i).start()
    unit = jnp.where(iota((wide, wide), 0) == iota((wide, wide), 1), 1.0, 0.0).astype(BF16)

    def turned(block):
        return lax.dot_general(unit, block, NT, preferred_element_type=F32)

    rim = turned(rim_ref[...])
    for i in range(cells // chunk):
        fetch(i).wait()
        for x in range(i * chunk // wide, (i + 1) * chunk // wide):
            at = x * wide * parts
            last = x == width_x - 1
            inside = x > 0 and not last
            if inside:
                start = x * wide - i * chunk
                block = turned(stage[i, :, start : start + wide])
            else:
                block = turned(ends_ref[int(last)])
            for c in range(parts):
                own = slice(c * 128, (c + 1) * 128)
                rows[pl.ds(at + c, wide, stride=parts), :] = block[:, own]
                if inside:
                    rows[at + c : at + c + 1, :] = rim[x : x + 1, own]
                    end = at + (wide - 1) * parts + c
                    rows[end : end + 1, :] = rim[wide // 2 + x : wide // 2 + x + 1, own]

    places.wait()
    share = picked.shape[1] // parts
    block = turned_out.shape[1]

    def row(at):
        return rows[pl.ds(pl.multiple_of(index_ref[at], parts), parts), :]

    def send(i):
        return pltpu.make_async_copy(
            turned_out.at[i % 2], out_hbm.at[i * block : (i + 1) * block], out_sems.at[i % 2]
        )

    for i in range(count // block):
        if i >= 2:
            send(i - 2).wait()

        def body(k, _):
            start = k * share
            slot = lax.rem(k, 2)
            source = piece * count + i * block + start
            for j in range(0, share, 2):
                pair = jnp.concatenate([row(source + j), row(source + j + 1)], axis=0)
                picked[slot, j * parts : (j + 2) * parts, :] = pair
            for c in range(parts):
                part = picked[slot, pl.ds(c, share, stride=parts), :]
                turned_out[
                    i % 2, pl.ds(pl.multiple_of(start, share), share), c * 128 : (c + 1) * 128
                ] = part.astype(BF16)
            return 0

        lax.fori_loop(0, block // share, body, 0)
        send(i).start()
    for i in range(max(count // block - 2, 0), count // block):
        send(i).wait()


def pick(piece, pieces, places, fields, rim, ends, after):
    columns, cells = fields.shape
    wide = rim.shape[1]
    parts = columns // 128
    share = 64
    block = next(n for n in (768, 512, 256, 128, 64) if cells % (pieces * n) == 0)
    chunk = next(n * wide for n in (8, 6, 4, 3, 2, 1) if cells % (n * wide) == 0)
    vmem = pl.BlockSpec(memory_space=pltpu.VMEM)
    hbm = pl.BlockSpec(memory_space=pl.ANY)
    return pl.pallas_call(
        functools.partial(pick_kernel, piece),
        in_specs=[hbm, hbm, vmem, vmem, hbm],
        out_specs=[hbm, vmem],
        out_shape=[jax.ShapeDtypeStruct((cells // pieces, columns), BF16), TOKEN],
        scratch_shapes=[
            pltpu.SMEM((cells,), jnp.int32),
            pltpu.VMEM((cells // chunk, columns, chunk), BF16),
            pltpu.VMEM((cells * parts, 128), F32),
            pltpu.VMEM((2, share * parts, 128), F32),
            pltpu.VMEM((2, block, columns), BF16),
            pltpu.SemaphoreType.DMA((cells // chunk,)),
            pltpu.SemaphoreType.DMA((3,)),
        ],
        compiler_params=pltpu.CompilerParams(vmem_limit_bytes=50 * MB),
        name="pick",
    )(places, fields, rim, ends, after)


def sublane(x, t):
    return jnp.broadcast_to(x[t : t + 1, :], x.shape)


def lane_of(x, t):
    at = jnp.full(x.shape, t, jnp.int32)
    return jnp.take_along_axis(x, at, axis=1, mode="promise_in_bounds")


def thirds(x):
    high = x.astype(BF16).astype(F32)
    rest = x - high
    middle = rest.astype(BF16).astype(F32)
    return high, middle, rest - middle


def eliminate(work, head, row):
    head = list(head)
    done = jnp.zeros_like(work)
    pivots = jnp.ones_like(work)
    for t in range(0, 8, 2):
        one, two = row == t, row == t + 1
        both = one | two
        a, b, c = sublane(head[t], t), sublane(head[t + 1], t), sublane(head[t + 1], t + 1)
        determinant = a * c - b * b
        inverse = 1.0 / determinant
        first = jnp.where(one, c, jnp.where(two, -b, head[t + 1] * b - head[t] * c))
        second = jnp.where(one, -b, jnp.where(two, a, head[t] * b - head[t + 1] * a))

        def apply(x):
            step = first * sublane(x, t) + second * sublane(x, t + 1)
            return jnp.where(both, 0.0, x) + step * inverse

        share = 1.0 / a
        upper, lower = sublane(work, t), sublane(work, t + 1)
        done = jnp.where(one, upper, jnp.where(two, lower - b * share * upper, done))
        pivots = jnp.where(one, a, jnp.where(two, determinant * share, pivots))
        for u in range(t + 2, 8):
            head[u] = apply(head[u])
        work = apply(work)
    return work, done, pivots


def inverse_factor(block, near=1):
    size = block.shape[0]
    count = size // 8
    lane = iota((8, size), 1)
    row = iota((8, size), 0)
    tiles = [block[8 * p : 8 * p + 8, :] for p in range(count)]
    out = []
    for p in range(count):
        base = 8 * p
        close = range(p + 1, min(p + 1 + near, count))
        cols = {q: [lane_of(tiles[q], base + t) for t in range(8)] for q in (p, *close)}
        own = (lane >= base) & (lane < base + 8)
        unit = jnp.where(lane == base + row, 1.0, 0.0)
        work, done, pivots = eliminate(jnp.where(own, unit, tiles[p]), cols[p], row)
        out.append(jnp.where(lane <= base + row, done * lax.rsqrt(pivots), 0.0))
        lines = [sublane(work, t) for t in range(8)]
        for q in close:
            terms = [cols[q][t] * lines[t] for t in range(8)]
            while len(terms) > 1:
                terms = [terms[i] + terms[i + 1] for i in range(0, len(terms), 2)]
            tiles[q] = jnp.where(own, 0.0, tiles[q]) - terms[0]
        if p + 1 + near < count:
            ah, am, al = thirds(jnp.where(lane >= base + 8 * (1 + near), tiles[p], 0.0))
            wh, wm, wl = thirds(work)
            left = jnp.concatenate([ah, ah, am, ah, al, am], axis=0).astype(BF16)
            right = jnp.concatenate([wh, wm, wh, wl, wh, wm], axis=0).astype(BF16)
            change = lax.dot_general(left, right, TN, preferred_element_type=F32)
            for q in range(p + 1 + near, count):
                tiles[q] = jnp.where(own, 0.0, tiles[q]) - change[8 * q : 8 * q + 8, :]
    return jnp.concatenate(out, axis=0)


def factor_kernel(
    scale, pieces_ref, rows_hbm, r_ref, basis_hbm, work, high_ref, low_ref, rows, stage, lead, sems
):
    columns = r_ref.shape[0]
    chunks, _, width = stage.shape[0], columns, stage.shape[2]
    steps = rows.shape[0] // width
    fetch = pltpu.make_async_copy(rows_hbm, rows, sems.at[chunks])
    fetch.start()
    opening = pltpu.make_async_copy(pieces_ref.at[0], lead, sems.at[chunks + 1])
    opening.start()
    opening.wait()
    size = pieces_ref.shape[1]
    count = columns // size
    same = iota((size, size), 0) == iota((size, size), 1)
    upper = iota((size, size), 0) <= iota((size, size), 1)

    def dot(a, b, dims):
        return lax.dot_general(
            a, b, dims, preferred_element_type=F32, precision=lax.Precision.HIGHEST
        )

    def piece(at):
        return pieces_ref[at] if at else lead[...]

    order = [(i, j) for i in range(count) for j in range(i, count)]
    across, along = [], []
    for i in range(count):
        diagonal = jnp.where(same, piece(order.index((i, i))), 0.0)
        across.append(lax.rsqrt(jnp.sum(diagonal, axis=0, keepdims=True)))
        along.append(lax.rsqrt(jnp.sum(diagonal, axis=1, keepdims=True)))
    for at, (i, j) in enumerate(order):
        work[i, j] = piece(at) * along[i] * across[j]

    def place(i, j):
        return slice(i * size, (i + 1) * size), slice(j * size, (j + 1) * size)

    for k in range(count):
        diagonal = work[k, k]
        inverse = inverse_factor(diagonal)
        for j in (*range(k + 1, count), *range(k)):
            work[k, j] = dot(inverse, work[k, j], NN)
        work[k, k] = inverse
        for i in range(k + 1, count):
            left = work[k, i]
            for j in (*range(i, count), *range(k + 1)):
                change = dot(left, work[k, j], TN)
                work[i, j] = -change if j == k else work[i, j] - change
        corner = jnp.where(upper, dot(inverse, diagonal, NN), 0.0)
        for j in range(count):
            known = work[k, j] * (across[j] * scale) if j <= k else jnp.zeros((size, size), F32)
            high = known.astype(BF16)
            high_ref[place(k, j)] = high
            low_ref[place(k, j)] = (known - high.astype(F32)).astype(BF16)
            grow = 1.0 / (across[j] * scale)
            r_ref[place(k, j)] = (
                corner * grow if j == k else work[k, j] * grow if j > k else jnp.zeros((size, size), F32)
            )

    fetch.wait()
    half = columns // 2

    def product(w, x):
        return lax.dot_general(w, x, NT, preferred_element_type=F32)

    def send(i):
        slot = lax.rem(i, chunks)
        place = pl.ds(pl.multiple_of(i * width, width), width)
        return pltpu.make_async_copy(stage.at[slot], basis_hbm.at[:, place], sems.at[slot])

    def body(i, _):
        slot = lax.rem(i, chunks)

        @pl.when(i >= chunks)
        def _():
            send(i - chunks).wait()

        block = rows[pl.ds(pl.multiple_of(i * width, width), width), :]
        first = block[:, :half]
        top = product(low_ref[:half, :half], first) + product(high_ref[:half, :half], first)
        stage[slot, :half, :] = top.astype(BF16)
        bottom = product(low_ref[half:, :], block) + product(high_ref[half:, :], block)
        stage[slot, half:, :] = bottom.astype(BF16)
        send(i).start()
        return 0

    lax.fori_loop(0, steps, body, 0)
    for i in range(max(steps - chunks, 0), steps):
        send(i).wait()


def factor(pieces, rows, columns, scale):
    vmem = pl.BlockSpec(memory_space=pltpu.VMEM)
    hbm = pl.BlockSpec(memory_space=pl.ANY)
    square = (columns, columns)
    size = pieces.shape[1]
    cells = rows.shape[0]
    width = next(n for n in (768, 512, 256, 128) if cells % n == 0)
    chunks = min(3, cells // width)
    return pl.pallas_call(
        functools.partial(factor_kernel, scale),
        in_specs=[vmem, hbm],
        out_specs=[vmem, hbm],
        out_shape=[
            jax.ShapeDtypeStruct(square, F32),
            jax.ShapeDtypeStruct((columns, cells), BF16),
        ],
        scratch_shapes=[
            pltpu.VMEM((columns // size, columns // size, size, size), F32),
            pltpu.VMEM(square, BF16),
            pltpu.VMEM(square, BF16),
            pltpu.VMEM((cells, columns), BF16),
            pltpu.VMEM((chunks, columns, width), BF16),
            pltpu.VMEM((size, size), F32),
            pltpu.SemaphoreType.DMA((chunks + 2,)),
        ],
        compiler_params=pltpu.CompilerParams(vmem_limit_bytes=50 * MB),
        name="factor",
    )(pieces, rows)


def shards(velocity, lon_metric, lat_metric, wet_index, wet_count):
    days = velocity.shape[1]
    cells = velocity.shape[2] * velocity.shape[3]
    columns = 2 * days
    lats, lons = lax.axis_size("lat"), lax.axis_size("lon")
    fields, total, lon, lat, south, second, north, before, fold, *outer = front(
        velocity, wet_index, wet_count, lon_metric, lat_metric
    )
    east_route = [(i, (i + 1) % lons) for i in range(lons)]
    west = lax.ppermute(outer[3], "lon", east_route)
    east = lax.ppermute(outer[0], "lon", [(t, s) for s, t in east_route])
    up = [(i, i + 1) for i in range(lats - 1)]
    below = lax.ppermute(north, "lat", up)
    above = lax.ppermute(south, "lat", [(t, s) for s, t in up])
    top = (lats - 1) * lons
    mirrored = lax.ppermute(fold, ("lat", "lon"), [(top + i, top + lons - 1 - i) for i in range(lons)])
    sides = (west, east, below, above, mirrored)
    edges = (south, second, north, before)
    gram, rows, ends = rim(outer, sides, edges, lon, lat, total, min(128, columns))

    places = wet_index * (columns // 128)
    pieces = 1
    held = {}

    def picking(piece, after):
        held[piece], token = pick(piece, pieces, places, fields, rows, ends, after)
        return token

    beside = {2 + piece: functools.partial(picking, piece) for piece in range(pieces)}
    total = all_sum(gram, beside)
    scale = math.sqrt(cells * lats * lons)
    triangle, basis = factor(total, held[0], columns, scale)
    return basis, triangle


def solution(mesh):
    placed = (
        P(None, None, "lon", "lat"),
        P("lon", "lat"),
        P("lon", "lat"),
        P(("lat", "lon")),
        P(("lat", "lon")),
    )
    return jax.shard_map(
        shards,
        mesh=mesh,
        in_specs=placed,
        out_specs=(P(None, ("lat", "lon")), P()),
        check_vma=False,
    )
```

```python
import functools
import math

import jax
import jax.numpy as jnp
from jax import lax
from jax.experimental import pallas as pl
from jax.experimental.pallas import tpu as pltpu
from jax.sharding import PartitionSpec as P

F32 = jnp.float32
BF16 = jnp.bfloat16
MB = 1 << 20
ROOM = 24 * MB
TOKEN = jax.ShapeDtypeStruct((8, 128), F32)
NN = (((1,), (0,)), ((), ()))
NT = (((1,), (1,)), ((), ()))
TN = (((0,), (0,)), ((), ()))


def iota(shape, dim):
    return lax.broadcasted_iota(jnp.int32, shape, dim)


def lat_difference(width_y):
    wide = 2 * width_y
    k = iota((wide, wide), 0)
    n = iota((wide, wide), 1)
    same = k // width_y == n // width_y
    diff = jnp.where(same & (k == n + 1), 1.0, 0.0) - jnp.where(same & (k == n - 1), 1.0, 0.0)
    return diff.astype(BF16)


def gram_of(block, days):
    upper = lax.dot_general(block[:days, :], block, NT, preferred_element_type=F32)
    lower = lax.dot_general(block[days:, :], block[days:, :], NT, preferred_element_type=F32)
    return upper, lower


def front_kernel(
    v_hbm, cells_ref, count_ref,
    fields_hbm, total, lon_out, lat_out, south_ref, second_ref, north_ref, before_ref, near_ref, far_ref,
    x0_ref, x1_ref, x2_ref, x3_ref, flag_ref,
    raw, moved, stage, lon_in, lat_in, sems, out_sems,
):
    fields, days, width_x, width_y = v_hbm.shape
    step = raw.shape[2]
    half = width_y // 2

    def fetch(i):
        return pltpu.make_async_copy(
            v_hbm.at[:, pl.ds(i * step, step)], raw.at[i], sems.at[i]
        )

    for i in range(days // step):
        fetch(i).start()

    cells = width_x * width_y
    index = cells_ref[2].astype(jnp.int32)
    index = jnp.concatenate([index[x : x + 1, :] for x in range(width_x)], axis=1)
    wet = iota(index.shape, 1) < count_ref[0]
    row = jnp.where(wet, index // width_y, -1)
    col = index % width_y
    pick_x = jnp.where(iota((width_x, cells), 0) == row, 1.0, 0.0).astype(BF16)
    pick_y = jnp.where(iota((width_y, cells), 0) == col, 1.0, 0.0).astype(BF16)
    mask = lax.dot_general(pick_x, pick_y, NT, preferred_element_type=F32)
    at_x = iota((width_x, width_y), 0)
    at_y = iota((width_x, width_y), 1)
    inner = (at_x > 0) & (at_x < width_x - 1) & (at_y > 0) & (at_y < width_y - 1)
    lon = 0.5 * cells_ref[0] * mask
    lat = 0.5 * cells_ref[1] * mask
    lon_out[...] = lon
    lat_out[...] = lat
    lon_in[...] = jnp.where(inner, lon, 0.0)
    lat_in[...] = jnp.where(inner, lat, 0.0)

    lane = iota((16, width_y), 1)

    def turn(i, _):
        fetch(i).wait()
        for d in range(0, step, 16):
            south = second = north = before = jnp.zeros((16, width_y), BF16)
            rows = pl.ds(pl.multiple_of(i * step + d, 16), 16)
            for f in range(fields):
                columns = jnp.swapaxes(raw[i, f, d : d + 16], 0, 1)
                moved[f, :, rows, :] = columns
                for x in range(width_x):
                    at = f * half + x
                    turned = pltpu.roll(columns[x], at + 1, 1)
                    before = jnp.where(lane == (at - 1) % width_y, turned, before)
                    north = jnp.where(lane == at, turned, north)
                    south = jnp.where(lane == at + 1, turned, south)
                    second = jnp.where(lane == at + 2, turned, second)
            south_ref[rows, :] = pltpu.roll(south, width_y - 1, 1)
            second_ref[rows, :] = pltpu.roll(second, width_y - 2, 1)
            north_ref[rows, :] = north
            before_ref[rows, :] = pltpu.roll(before, 1, 1)
        return 0

    lax.fori_loop(0, days // step, turn, 0)
    k = iota((width_y, width_y), 0)
    n = iota((width_y, width_y), 1)
    mirror = (k // half == n // half) & (k + n == 2 * half * (n // half) + width_x - 1)
    mirror = jnp.where(mirror, -1.0, 0.0).astype(BF16)
    fold = lax.dot_general(north_ref[...], mirror, NN, preferred_element_type=F32)
    flag = cells_ref[3, :1, :]
    flag_ref[...] = cells_ref[3, :8, :]
    odd, top = flag % 2 == 1, flag >= 2
    south, north = south_ref[...].astype(F32), north_ref[...].astype(F32)
    near_ref[...] = jnp.where(odd, south, north).astype(BF16)
    far_ref[...] = jnp.where(top, fold, jnp.where(odd, north, south)).astype(BF16)
    x0_ref[...] = moved[:, 0]
    x1_ref[...] = moved[:, 1]
    x2_ref[...] = moved[:, width_x - 2]
    x3_ref[...] = moved[:, width_x - 1]

    wide = stage.shape[2]
    group = wide // width_y
    steps = width_x // group
    diff = lat_difference(width_y)
    total[...] = jnp.zeros_like(total)

    def send(i):
        slot = lax.rem(i, 2)
        place = pl.ds(pl.multiple_of(i * wide, wide), wide)
        return pltpu.make_async_copy(stage.at[slot], fields_hbm.at[:, place], out_sems.at[slot])

    def compute(i, _):
        slot = lax.rem(i, 2)

        @pl.when(i >= 2)
        def _():
            send(i - 2).wait()

        for g in range(group):
            x = i * group + g
            east = jnp.minimum(x + 1, width_x - 1)
            west = jnp.maximum(x - 1, 0)
            here = jnp.concatenate([moved[0, x], moved[1, x]], axis=1)
            along = lax.dot_general(here, diff, NN, preferred_element_type=F32)
            lon = lon_in[pl.ds(x, 1), :]
            lat = lat_in[pl.ds(x, 1), :]
            across_u = moved[0, east].astype(F32) - moved[0, west].astype(F32)
            across_v = moved[1, east].astype(F32) - moved[1, west].astype(F32)
            zeta = lon * across_v - lat * along[:, :width_y]
            divergence = lon * across_u + lat * along[:, width_y:]
            place = slice(g * width_y, (g + 1) * width_y)
            stage[slot, :days, place] = zeta.astype(BF16)
            stage[slot, days:, place] = divergence.astype(BF16)
        send(i).start()
        upper, lower = gram_of(stage[slot], days)
        total[:days, :] += upper
        total[days:, days:] += lower
        return 0

    lax.fori_loop(0, steps, compute, 0)
    for i in range(max(steps - 2, 0), steps):
        send(i).wait()


def front(velocity, wet_index, wet_count, lon_metric, lat_metric, flag):
    fields, days, width_x, width_y = velocity.shape
    assert width_x <= width_y // 2 - 2
    step = next(n for n in (32, 16) if days % n == 0)
    places = wet_index.reshape(width_x, width_y).astype(F32)
    group = next(n for n in (8, 6, 4, 3, 2, 1) if width_x % n == 0)
    vmem = pl.BlockSpec(memory_space=pltpu.VMEM)
    hbm = pl.BlockSpec(memory_space=pl.ANY)
    metric = jax.ShapeDtypeStruct((width_x, width_y), F32)
    edge = jax.ShapeDtypeStruct((days, width_y), BF16)
    column = jax.ShapeDtypeStruct((fields, days, width_y), BF16)
    return pl.pallas_call(
        front_kernel,
        in_specs=[hbm, vmem, pl.BlockSpec(memory_space=pltpu.SMEM)],
        out_specs=[hbm] + [vmem] * 14,
        out_shape=[
            jax.ShapeDtypeStruct((2 * days, width_x * width_y), BF16),
            jax.ShapeDtypeStruct((2 * days, 2 * days), F32),
            metric, metric, *[edge] * 6, *[column] * 4, jax.ShapeDtypeStruct((8, width_y), F32),
        ],
        scratch_shapes=[
            pltpu.VMEM((days // step, fields, step, width_x, width_y), BF16),
            pltpu.VMEM((fields, width_x, days, width_y), BF16),
            pltpu.VMEM((2, 2 * days, group * width_y), BF16),
            pltpu.VMEM((width_x, width_y), F32),
            pltpu.VMEM((width_x, width_y), F32),
            pltpu.SemaphoreType.DMA((days // step,)),
            pltpu.SemaphoreType.DMA((2,)),
        ],
        compiler_params=pltpu.CompilerParams(vmem_limit_bytes=50 * MB),
        name="front",
    )(velocity, jnp.stack([lon_metric, lat_metric, places, jnp.full_like(places, flag)]), wet_count)


def rim_kernel(
    x0_ref, x1_ref, x2_ref, x3_ref, west_ref, east_ref, near_ref, far_ref, flag_ref,
    south_ref, second_ref, north_ref, before_ref, lon_ref, lat_ref, total_ref,
    gram_ref, rows_ref, ends_ref,
):
    _, days, width_y = x0_ref.shape
    width_x = lon_ref.shape[0]
    half = width_y // 2
    odd = flag_ref[:1, :] % 2 == 1
    near, far = near_ref[...].astype(F32), far_ref[...].astype(F32)
    below, above = jnp.where(odd, near, far), jnp.where(odd, far, near)
    lane = iota((1, width_y), 1)

    diff = lat_difference(width_y)
    column_lane = iota((days, width_y), 1)
    for end, x, own_ref, west, east in (
        (0, 0, x0_ref, west_ref, x1_ref),
        (1, width_x - 1, x3_ref, x2_ref, east_ref),
    ):
        here = jnp.concatenate([own_ref[0], own_ref[1]], axis=1)
        along = lax.dot_general(here, diff, NN, preferred_element_type=F32)
        lon = lon_ref[x : x + 1, :]
        lat = lat_ref[x : x + 1, :]
        flow = []
        for f in range(2):
            own = along[:, f * width_y : (f + 1) * width_y]
            at = f * half + x
            own = own - jnp.where(column_lane == 0, below[:, at : at + 1], 0.0)
            own = own + jnp.where(column_lane == width_y - 1, above[:, at : at + 1], 0.0)
            flow.append(own)
        across_u = east[0].astype(F32) - west[0].astype(F32)
        across_v = east[1].astype(F32) - west[1].astype(F32)
        ends_ref[end, :days, :] = (lon * across_v - lat * flow[0]).astype(BF16)
        ends_ref[end, days:, :] = (lon * across_u + lat * flow[1]).astype(BF16)

    fill = jnp.zeros((width_y - width_x, width_y), F32)
    lon_turned = jnp.concatenate([lon_ref[...], fill], axis=0).T
    lat_turned = jnp.concatenate([lat_ref[...], fill], axis=0).T
    spot = lane % half
    between = (spot > 0) & (spot < width_x - 1)
    parts = []
    for y, row, low, high in (
        (0, south_ref, below, second_ref[...].astype(F32)),
        (width_y - 1, north_ref, before_ref[...].astype(F32), above),
    ):
        lon = lon_turned[y : y + 1, :]
        lat = lat_turned[y : y + 1, :]
        lon = jnp.where(between, jnp.where(lane < half, lon, pltpu.roll(lon, half, 1)), 0.0)
        lat = jnp.where(between, jnp.where(lane < half, -lat, pltpu.roll(lat, half, 1)), 0.0)
        own = row[...].astype(F32)
        across = pltpu.roll(own, width_y - 1, 1) - pltpu.roll(own, 1, 1)
        parts.append(lon * pltpu.roll(across, half, 1) + lat * (high - low))
    low_lane = column_lane < half
    rows_ref[:days, :] = jnp.where(low_lane, parts[0], pltpu.roll(parts[1], half, 1)).astype(BF16)
    rows_ref[days:, :] = jnp.where(low_lane, pltpu.roll(parts[0], half, 1), parts[1]).astype(BF16)

    rim = jnp.concatenate([ends_ref[0], ends_ref[1], rows_ref[...]], axis=1)
    upper, lower = gram_of(rim, days)
    size = gram_ref.shape[1]
    at = 0
    for i in range(2 * days // size):
        for j in range(i, 2 * days // size):
            left = slice(i * size, (i + 1) * size)
            right = slice(j * size, (j + 1) * size)
            if i * size < days:
                extra = upper[left, right]
            else:
                extra = lower[
                    i * size - days : (i + 1) * size - days, j * size - days : (j + 1) * size - days
                ]
            gram_ref[at] = total_ref[left, right] + extra
            at += 1


def rim(ends, sides, edges, lon, lat, total, size):
    _, days, width_y = ends[0].shape
    count = 2 * days // size
    vmem = pl.BlockSpec(memory_space=pltpu.VMEM)
    operands = (*ends, *sides, *edges, lon, lat, total)
    return pl.pallas_call(
        rim_kernel,
        in_specs=[vmem] * len(operands),
        out_specs=[vmem] * 3,
        out_shape=[
            jax.ShapeDtypeStruct((count * (count + 1) // 2, size, size), F32),
            jax.ShapeDtypeStruct((2 * days, width_y), BF16),
            jax.ShapeDtypeStruct((2, 2 * days, width_y), BF16),
        ],
        compiler_params=pltpu.CompilerParams(vmem_limit_bytes=ROOM),
        name="rim",
    )(*operands)


def all_sum(x, beside):
    moves = []
    for axis in ("lat", "lon"):
        count = lax.axis_size(axis)
        assert count & (count - 1) == 0
        for bit in range(count.bit_length() - 1):
            moves.append((axis, bit))
    shape = x.shape
    x = x.reshape(-1, shape[-1])
    taken = []

    hops = 0

    def swap(block, axis, bit):
        nonlocal hops
        other = lax.ppermute(
            block, axis, [(i, i ^ 1 << bit) for i in range(lax.axis_size(axis))]
        )
        if hops in beside:
            other = other + beside[hops](block)[0, 0]
        hops += 1
        return other

    for axis, bit in moves:
        halve = x.shape[0] % 16 == 0 and x.shape[0] > shape[0] * 16
        if halve:
            half = x.shape[0] // 2
            high = (lax.axis_index(axis) >> bit) & 1
            keep = lax.dynamic_slice_in_dim(x, high * half, half, 0)
            send = lax.dynamic_slice_in_dim(x, (1 - high) * half, half, 0)
            x = keep + swap(send, axis, bit)
        else:
            x = x + swap(x, axis, bit)
        taken.append(halve)
    for (axis, bit), halve in reversed(list(zip(moves, taken))):
        if halve:
            high = (lax.axis_index(axis) >> bit) & 1
            other = swap(x, axis, bit)
            x = jnp.where(
                high == 1, jnp.concatenate([other, x], 0), jnp.concatenate([x, other], 0)
            )
    return x.reshape(shape)


def pick_kernel(
    piece, share, index_hbm, fields_hbm, rim_ref, ends_ref, after_ref, out_hbm, token_ref,
    index_ref, stage, rows, picked, turned_out, sems, out_sems,
):
    token_ref[...] = jnp.zeros_like(token_ref)
    columns, wide = rim_ref.shape
    count = out_hbm.shape[0]
    cells = fields_hbm.shape[1]
    width_x = cells // wide
    parts = columns // 128
    chunk = stage.shape[2]

    def fetch(i):
        return pltpu.make_async_copy(
            fields_hbm.at[:, i * chunk : (i + 1) * chunk], stage.at[i], sems.at[i]
        )

    places = pltpu.make_async_copy(index_hbm, index_ref, out_sems.at[2])
    places.start()
    for i in range(cells // chunk):
        fetch(i).start()
    unit = jnp.where(iota((wide, wide), 0) == iota((wide, wide), 1), 1.0, 0.0).astype(BF16)

    def turned(block):
        return lax.dot_general(unit, block, NT, preferred_element_type=F32)

    rim = turned(rim_ref[...])
    for i in range(cells // chunk):
        fetch(i).wait()
        for x in range(i * chunk // wide, (i + 1) * chunk // wide):
            at = x * wide * parts
            last = x == width_x - 1
            inside = x > 0 and not last
            if inside:
                start = x * wide - i * chunk
                block = turned(stage[i, :, start : start + wide])
            else:
                block = turned(ends_ref[int(last)])
            for c in range(parts):
                own = slice(c * 128, (c + 1) * 128)
                rows[pl.ds(at + c, wide, stride=parts), :] = block[:, own]
                if inside:
                    rows[at + c : at + c + 1, :] = rim[x : x + 1, own]
                    end = at + (wide - 1) * parts + c
                    rows[end : end + 1, :] = rim[wide // 2 + x : wide // 2 + x + 1, own]

    places.wait()
    block = turned_out.shape[1]

    def row(at):
        return rows[pl.ds(pl.multiple_of(index_ref[at], parts), parts), :]

    def send(i):
        return pltpu.make_async_copy(
            turned_out.at[i % 2], out_hbm.at[i * block : (i + 1) * block], out_sems.at[i % 2]
        )

    for i in range(count // block):
        if i >= 2:
            send(i - 2).wait()

        def body(k, _):
            start = k * share
            slot = lax.rem(k, 2)
            source = piece * count + i * block + start
            for j in range(0, share, 2):
                pair = jnp.concatenate([row(source + j), row(source + j + 1)], axis=0)
                picked[slot, j * parts : (j + 2) * parts, :] = pair
            for c in range(parts):
                part = picked[slot, pl.ds(c, share, stride=parts), :]
                turned_out[
                    i % 2, pl.ds(pl.multiple_of(start, share), share), c * 128 : (c + 1) * 128
                ] = part.astype(BF16)
            return 0

        lax.fori_loop(0, block // share, body, 0)
        send(i).start()
    for i in range(max(count // block - 2, 0), count // block):
        send(i).wait()


def pick(piece, pieces, places, fields, rim, ends, after):
    columns, cells = fields.shape
    wide = rim.shape[1]
    parts = columns // 128
    share = 64
    block = next(n for n in (768, 512, 256, 128, 64) if cells % (pieces * n) == 0)
    chunk = next(n * wide for n in (8, 6, 4, 3, 2, 1) if cells % (n * wide) == 0)
    vmem = pl.BlockSpec(memory_space=pltpu.VMEM)
    hbm = pl.BlockSpec(memory_space=pl.ANY)
    return pl.pallas_call(
        functools.partial(pick_kernel, piece, share),
        in_specs=[hbm, hbm, vmem, vmem, hbm],
        out_specs=[hbm, vmem],
        out_shape=[jax.ShapeDtypeStruct((cells // pieces, columns), BF16), TOKEN],
        scratch_shapes=[
            pltpu.SMEM((cells,), jnp.int32),
            pltpu.VMEM((cells // chunk, columns, chunk), BF16),
            pltpu.VMEM((cells * parts + 8, 128), F32),
            pltpu.VMEM((2, share * parts + 8, 128), F32),
            pltpu.VMEM((2, block, columns), BF16),
            pltpu.SemaphoreType.DMA((cells // chunk,)),
            pltpu.SemaphoreType.DMA((3,)),
        ],
        compiler_params=pltpu.CompilerParams(vmem_limit_bytes=50 * MB),
        name="pick",
    )(places, fields, rim, ends, after)


def sublane(x, t):
    return jnp.broadcast_to(x[t : t + 1, :], x.shape)


def lane_of(x, t):
    at = jnp.full(x.shape, t, jnp.int32)
    return jnp.take_along_axis(x, at, axis=1, mode="promise_in_bounds")


def thirds(x):
    high = x.astype(BF16).astype(F32)
    rest = x - high
    middle = rest.astype(BF16).astype(F32)
    return high, middle, rest - middle


def eliminate(work, head, row):
    head = list(head)
    done = jnp.zeros_like(work)
    pivots = jnp.ones_like(work)
    for t in range(0, 8, 2):
        one, two = row == t, row == t + 1
        both = one | two
        a, b, c = sublane(head[t], t), sublane(head[t + 1], t), sublane(head[t + 1], t + 1)
        determinant = a * c - b * b
        inverse = 1.0 / determinant
        first = jnp.where(one, c, jnp.where(two, -b, head[t + 1] * b - head[t] * c))
        second = jnp.where(one, -b, jnp.where(two, a, head[t] * b - head[t + 1] * a))

        def apply(x):
            step = first * sublane(x, t) + second * sublane(x, t + 1)
            return jnp.where(both, 0.0, x) + step * inverse

        share = 1.0 / a
        upper, lower = sublane(work, t), sublane(work, t + 1)
        done = jnp.where(one, upper, jnp.where(two, lower - b * share * upper, done))
        pivots = jnp.where(one, a, jnp.where(two, determinant * share, pivots))
        for u in range(t + 2, 8):
            head[u] = apply(head[u])
        work = apply(work)
    return work, done, pivots


def inverse_factor(block, near=1):
    size = block.shape[0]
    count = size // 8
    lane = iota((8, size), 1)
    row = iota((8, size), 0)
    tiles = [block[8 * p : 8 * p + 8, :] for p in range(count)]
    out = []
    for p in range(count):
        base = 8 * p
        close = range(p + 1, min(p + 1 + near, count))
        cols = {q: [lane_of(tiles[q], base + t) for t in range(8)] for q in (p, *close)}
        own = (lane >= base) & (lane < base + 8)
        unit = jnp.where(lane == base + row, 1.0, 0.0)
        work, done, pivots = eliminate(jnp.where(own, unit, tiles[p]), cols[p], row)
        out.append(jnp.where(lane <= base + row, done * lax.rsqrt(pivots), 0.0))
        lines = [sublane(work, t) for t in range(8)]
        for q in close:
            terms = [cols[q][t] * lines[t] for t in range(8)]
            while len(terms) > 1:
                terms = [terms[i] + terms[i + 1] for i in range(0, len(terms), 2)]
            tiles[q] = jnp.where(own, 0.0, tiles[q]) - terms[0]
        if p + 1 + near < count:
            ah, am, al = thirds(jnp.where(lane >= base + 8 * (1 + near), tiles[p], 0.0))
            wh, wm, wl = thirds(work)
            left = jnp.concatenate([ah, ah, am, ah, al, am], axis=0).astype(BF16)
            right = jnp.concatenate([wh, wm, wh, wl, wh, wm], axis=0).astype(BF16)
            change = lax.dot_general(left, right, TN, preferred_element_type=F32)
            for q in range(p + 1 + near, count):
                tiles[q] = jnp.where(own, 0.0, tiles[q]) - change[8 * q : 8 * q + 8, :]
    return jnp.concatenate(out, axis=0)


def factor_kernel(
    scale, pieces_ref, rows_hbm, r_ref, basis_hbm, work, high_ref, low_ref, rows, stage, lead, sems
):
    columns = r_ref.shape[0]
    chunks, _, width = stage.shape[0], columns, stage.shape[2]
    steps = rows.shape[0] // width
    fetch = pltpu.make_async_copy(rows_hbm, rows, sems.at[chunks])
    fetch.start()
    opening = pltpu.make_async_copy(pieces_ref.at[0], lead, sems.at[chunks + 1])
    opening.start()
    opening.wait()
    size = pieces_ref.shape[1]
    count = columns // size
    same = iota((size, size), 0) == iota((size, size), 1)
    upper = iota((size, size), 0) <= iota((size, size), 1)

    def dot(a, b, dims):
        return lax.dot_general(
            a, b, dims, preferred_element_type=F32, precision=lax.Precision.HIGHEST
        )

    def piece(at):
        return pieces_ref[at] if at else lead[...]

    order = [(i, j) for i in range(count) for j in range(i, count)]
    across, along = [], []
    for i in range(count):
        diagonal = jnp.where(same, piece(order.index((i, i))), 0.0)
        across.append(lax.rsqrt(jnp.sum(diagonal, axis=0, keepdims=True)))
        along.append(lax.rsqrt(jnp.sum(diagonal, axis=1, keepdims=True)))
    for at, (i, j) in enumerate(order):
        work[i, j] = piece(at) * along[i] * across[j]

    def place(i, j):
        return slice(i * size, (i + 1) * size), slice(j * size, (j + 1) * size)

    for k in range(count):
        diagonal = work[k, k]
        inverse = inverse_factor(diagonal)
        for j in (*range(k + 1, count), *range(k)):
            work[k, j] = dot(inverse, work[k, j], NN)
        work[k, k] = inverse
        for i in range(k + 1, count):
            left = work[k, i]
            for j in (*range(i, count), *range(k + 1)):
                change = dot(left, work[k, j], TN)
                work[i, j] = -change if j == k else work[i, j] - change
        corner = jnp.where(upper, dot(inverse, diagonal, NN), 0.0)
        for j in range(count):
            known = work[k, j] * (across[j] * scale) if j <= k else jnp.zeros((size, size), F32)
            high = known.astype(BF16)
            high_ref[place(k, j)] = high
            low_ref[place(k, j)] = (known - high.astype(F32)).astype(BF16)
            grow = 1.0 / (across[j] * scale)
            r_ref[place(k, j)] = (
                corner * grow if j == k else work[k, j] * grow if j > k else jnp.zeros((size, size), F32)
            )

    fetch.wait()
    half = columns // 2

    def product(w, x):
        return lax.dot_general(w, x, NT, preferred_element_type=F32)

    def send(i):
        slot = lax.rem(i, chunks)
        place = pl.ds(pl.multiple_of(i * width, width), width)
        return pltpu.make_async_copy(stage.at[slot], basis_hbm.at[:, place], sems.at[slot])

    def body(i, _):
        slot = lax.rem(i, chunks)

        @pl.when(i >= chunks)
        def _():
            send(i - chunks).wait()

        block = rows[pl.ds(pl.multiple_of(i * width, width), width), :]
        first = block[:, :half]
        top = product(low_ref[:half, :half], first) + product(high_ref[:half, :half], first)
        stage[slot, :half, :] = top.astype(BF16)
        bottom = product(low_ref[half:, :], block) + product(high_ref[half:, :], block)
        stage[slot, half:, :] = bottom.astype(BF16)
        send(i).start()
        return 0

    lax.fori_loop(0, steps, body, 0)
    for i in range(max(steps - chunks, 0), steps):
        send(i).wait()


def factor(pieces, rows, columns, scale):
    vmem = pl.BlockSpec(memory_space=pltpu.VMEM)
    hbm = pl.BlockSpec(memory_space=pl.ANY)
    square = (columns, columns)
    size = pieces.shape[1]
    cells = rows.shape[0]
    width = next(n for n in (768, 512, 256, 128) if cells % n == 0)
    chunks = min(3, cells // width)
    return pl.pallas_call(
        functools.partial(factor_kernel, scale),
        in_specs=[vmem, hbm],
        out_specs=[vmem, hbm],
        out_shape=[
            jax.ShapeDtypeStruct(square, F32),
            jax.ShapeDtypeStruct((columns, cells), BF16),
        ],
        scratch_shapes=[
            pltpu.VMEM((columns // size, columns // size, size, size), F32),
            pltpu.VMEM(square, BF16),
            pltpu.VMEM(square, BF16),
            pltpu.VMEM((cells, columns), BF16),
            pltpu.VMEM((chunks, columns, width), BF16),
            pltpu.VMEM((size, size), F32),
            pltpu.SemaphoreType.DMA((chunks + 2,)),
        ],
        compiler_params=pltpu.CompilerParams(vmem_limit_bytes=50 * MB),
        name="factor",
    )(pieces, rows)


def shards(velocity, lon_metric, lat_metric, wet_index, wet_count):
    days = velocity.shape[1]
    cells = velocity.shape[2] * velocity.shape[3]
    columns = 2 * days
    lats, lons = lax.axis_size("lat"), lax.axis_size("lon")
    row = lax.axis_index("lat")
    flag = (row % 2 + 2 * (row == lats - 1)).astype(F32)
    fields, total, lon, lat, south, second, north, before, near, far, *outer, flag = front(
        velocity, wet_index, wet_count, lon_metric, lat_metric, flag
    )
    east_route = [(i, (i + 1) % lons) for i in range(lons)]
    west = lax.ppermute(outer[3], "lon", east_route)
    east = lax.ppermute(outer[0], "lon", [(t, s) for s, t in east_route])
    assert lats % 2 == 0
    near = lax.ppermute(near, "lat", [(i, i ^ 1) for i in range(lats)])
    route = []
    for x in range(lons):
        for y in range(1, lats - 1):
            other = y + 1 if y % 2 else y - 1
            route.append((y * lons + x, other * lons + x))
        route.append(((lats - 1) * lons + x, lats * lons - 1 - x))
    far = lax.ppermute(far, ("lat", "lon"), route)
    sides = (west, east, near, far, flag)
    cells_in_order, lon = lax.optimization_barrier((wet_index, lon))
    places = cells_in_order * (columns // 128)
    edges = (south, second, north, before)
    gram, rows, ends = rim(outer, sides, edges, lon, lat, total, min(128, columns))

    pieces = 1
    held = {}

    def picking(piece, after):
        held[piece], token = pick(piece, pieces, places, fields, rows, ends, after)
        return token

    beside = {2 + piece: functools.partial(picking, piece) for piece in range(pieces)}
    total = all_sum(gram, beside)
    scale = math.sqrt(cells * lats * lons)
    triangle, basis = factor(total, held[0], columns, scale)
    return basis, triangle


def solution(mesh):
    placed = (
        P(None, None, "lon", "lat"),
        P("lon", "lat"),
        P("lon", "lat"),
        P(("lat", "lon")),
        P(("lat", "lon")),
    )
    return jax.shard_map(
        shards,
        mesh=mesh,
        in_specs=placed,
        out_specs=(P(None, ("lat", "lon")), P()),
        check_vma=False,
    )
```

```python
import functools
import math

import jax
import jax.numpy as jnp
from jax import lax
from jax.experimental import pallas as pl
from jax.experimental.pallas import tpu as pltpu
from jax.sharding import PartitionSpec as P

F32 = jnp.float32
BF16 = jnp.bfloat16
MB = 1 << 20
ROOM = 24 * MB
TOKEN = jax.ShapeDtypeStruct((8, 128), F32)
NN = (((1,), (0,)), ((), ()))
NT = (((1,), (1,)), ((), ()))
TN = (((0,), (0,)), ((), ()))


def iota(shape, dim):
    return lax.broadcasted_iota(jnp.int32, shape, dim)


def lat_difference(width_y):
    wide = 2 * width_y
    k = iota((wide, wide), 0)
    n = iota((wide, wide), 1)
    same = k // width_y == n // width_y
    diff = jnp.where(same & (k == n + 1), 1.0, 0.0) - jnp.where(same & (k == n - 1), 1.0, 0.0)
    return diff.astype(BF16)


def gram_of(block, days):
    upper = lax.dot_general(block[:days, :], block, NT, preferred_element_type=F32)
    lower = lax.dot_general(block[days:, :], block[days:, :], NT, preferred_element_type=F32)
    return upper, lower


def front_kernel(
    v_hbm, cells_ref, count_ref,
    fields_hbm, total, lon_out, lat_out, south_ref, second_ref, north_ref, before_ref, near_ref, far_ref,
    x0_ref, x1_ref, x2_ref, x3_ref, flag_ref,
    raw, moved, stage, lon_in, lat_in, sems, out_sems,
):
    fields, days, width_x, width_y = v_hbm.shape
    step = raw.shape[2]
    half = width_y // 2

    def fetch(i):
        return pltpu.make_async_copy(
            v_hbm.at[:, pl.ds(i * step, step)], raw.at[i], sems.at[i]
        )

    for i in range(days // step):
        fetch(i).start()

    cells = width_x * width_y
    index = cells_ref[2].astype(jnp.int32)
    index = jnp.concatenate([index[x : x + 1, :] for x in range(width_x)], axis=1)
    wet = iota(index.shape, 1) < count_ref[0]
    row = jnp.where(wet, index // width_y, -1)
    col = index % width_y
    pick_x = jnp.where(iota((width_x, cells), 0) == row, 1.0, 0.0).astype(BF16)
    pick_y = jnp.where(iota((width_y, cells), 0) == col, 1.0, 0.0).astype(BF16)
    mask = lax.dot_general(pick_x, pick_y, NT, preferred_element_type=F32)
    at_x = iota((width_x, width_y), 0)
    at_y = iota((width_x, width_y), 1)
    inner = (at_x > 0) & (at_x < width_x - 1) & (at_y > 0) & (at_y < width_y - 1)
    lon = 0.5 * cells_ref[0] * mask
    lat = 0.5 * cells_ref[1] * mask
    lon_out[...] = lon
    lat_out[...] = lat
    lon_in[...] = jnp.where(inner, lon, 0.0)
    lat_in[...] = jnp.where(inner, lat, 0.0)

    lane = iota((16, width_y), 1)

    def turn(i, _):
        fetch(i).wait()
        for d in range(0, step, 16):
            south = second = north = before = jnp.zeros((16, width_y), BF16)
            rows = pl.ds(pl.multiple_of(i * step + d, 16), 16)
            for f in range(fields):
                columns = jnp.swapaxes(raw[i, f, d : d + 16], 0, 1)
                moved[f, :, rows, :] = columns
                for x in range(width_x):
                    at = f * half + x
                    turned = pltpu.roll(columns[x], at + 1, 1)
                    before = jnp.where(lane == (at - 1) % width_y, turned, before)
                    north = jnp.where(lane == at, turned, north)
                    south = jnp.where(lane == at + 1, turned, south)
                    second = jnp.where(lane == at + 2, turned, second)
            south_ref[rows, :] = pltpu.roll(south, width_y - 1, 1)
            second_ref[rows, :] = pltpu.roll(second, width_y - 2, 1)
            north_ref[rows, :] = north
            before_ref[rows, :] = pltpu.roll(before, 1, 1)
        return 0

    lax.fori_loop(0, days // step, turn, 0)
    k = iota((width_y, width_y), 0)
    n = iota((width_y, width_y), 1)
    mirror = (k // half == n // half) & (k + n == 2 * half * (n // half) + width_x - 1)
    mirror = jnp.where(mirror, -1.0, 0.0).astype(BF16)
    fold = lax.dot_general(north_ref[...], mirror, NN, preferred_element_type=F32)
    flag = cells_ref[3, :1, :]
    flag_ref[...] = cells_ref[3, :8, :]
    odd, top = flag % 2 == 1, flag >= 2
    south, north = south_ref[...].astype(F32), north_ref[...].astype(F32)
    near_ref[...] = jnp.where(odd, south, north).astype(BF16)
    far_ref[...] = jnp.where(top, fold, jnp.where(odd, north, south)).astype(BF16)
    x0_ref[...] = moved[:, 0]
    x1_ref[...] = moved[:, 1]
    x2_ref[...] = moved[:, width_x - 2]
    x3_ref[...] = moved[:, width_x - 1]

    wide = stage.shape[2]
    group = wide // width_y
    steps = width_x // group
    diff = lat_difference(width_y)
    total[...] = jnp.zeros_like(total)

    def send(i):
        slot = lax.rem(i, 2)
        place = pl.ds(pl.multiple_of(i * wide, wide), wide)
        return pltpu.make_async_copy(stage.at[slot], fields_hbm.at[:, place], out_sems.at[slot])

    def compute(i, _):
        slot = lax.rem(i, 2)

        @pl.when(i >= 2)
        def _():
            send(i - 2).wait()

        for g in range(group):
            x = i * group + g
            east = jnp.minimum(x + 1, width_x - 1)
            west = jnp.maximum(x - 1, 0)
            here = jnp.concatenate([moved[0, x], moved[1, x]], axis=1)
            along = lax.dot_general(here, diff, NN, preferred_element_type=F32)
            lon = lon_in[pl.ds(x, 1), :]
            lat = lat_in[pl.ds(x, 1), :]
            across_u = moved[0, east].astype(F32) - moved[0, west].astype(F32)
            across_v = moved[1, east].astype(F32) - moved[1, west].astype(F32)
            zeta = lon * across_v - lat * along[:, :width_y]
            divergence = lon * across_u + lat * along[:, width_y:]
            place = slice(g * width_y, (g + 1) * width_y)
            stage[slot, :days, place] = zeta.astype(BF16)
            stage[slot, days:, place] = divergence.astype(BF16)
        send(i).start()
        upper, lower = gram_of(stage[slot], days)
        total[:days, :] += upper
        total[days:, days:] += lower
        return 0

    lax.fori_loop(0, steps, compute, 0)
    for i in range(max(steps - 2, 0), steps):
        send(i).wait()


def front(velocity, wet_index, wet_count, lon_metric, lat_metric, flag):
    fields, days, width_x, width_y = velocity.shape
    assert width_x <= width_y // 2 - 2
    step = next(n for n in (32, 16) if days % n == 0)
    places = wet_index.reshape(width_x, width_y).astype(F32)
    group = next(n for n in (8, 6, 4, 3, 2, 1) if width_x % n == 0)
    vmem = pl.BlockSpec(memory_space=pltpu.VMEM)
    hbm = pl.BlockSpec(memory_space=pl.ANY)
    metric = jax.ShapeDtypeStruct((width_x, width_y), F32)
    edge = jax.ShapeDtypeStruct((days, width_y), BF16)
    column = jax.ShapeDtypeStruct((fields, days, width_y), BF16)
    return pl.pallas_call(
        front_kernel,
        in_specs=[hbm, vmem, pl.BlockSpec(memory_space=pltpu.SMEM)],
        out_specs=[hbm] + [vmem] * 14,
        out_shape=[
            jax.ShapeDtypeStruct((2 * days, width_x * width_y), BF16),
            jax.ShapeDtypeStruct((2 * days, 2 * days), F32),
            metric, metric, *[edge] * 6, *[column] * 4, jax.ShapeDtypeStruct((8, width_y), F32),
        ],
        scratch_shapes=[
            pltpu.VMEM((days // step, fields, step, width_x, width_y), BF16),
            pltpu.VMEM((fields, width_x, days, width_y), BF16),
            pltpu.VMEM((2, 2 * days, group * width_y), BF16),
            pltpu.VMEM((width_x, width_y), F32),
            pltpu.VMEM((width_x, width_y), F32),
            pltpu.SemaphoreType.DMA((days // step,)),
            pltpu.SemaphoreType.DMA((2,)),
        ],
        compiler_params=pltpu.CompilerParams(vmem_limit_bytes=50 * MB),
        name="front",
    )(velocity, jnp.stack([lon_metric, lat_metric, places, jnp.full_like(places, flag)]), wet_count)


def rim_kernel(
    x0_ref, x1_ref, x2_ref, x3_ref, west_ref, east_ref, near_ref, far_ref, flag_ref,
    south_ref, second_ref, north_ref, before_ref, lon_ref, lat_ref, total_ref,
    gram_ref, rows_ref, ends_ref,
):
    _, days, width_y = x0_ref.shape
    width_x = lon_ref.shape[0]
    half = width_y // 2
    odd = flag_ref[:1, :] % 2 == 1
    near, far = near_ref[...].astype(F32), far_ref[...].astype(F32)
    below, above = jnp.where(odd, near, far), jnp.where(odd, far, near)
    lane = iota((1, width_y), 1)

    diff = lat_difference(width_y)
    column_lane = iota((days, width_y), 1)
    for end, x, own_ref, west, east in (
        (0, 0, x0_ref, west_ref, x1_ref),
        (1, width_x - 1, x3_ref, x2_ref, east_ref),
    ):
        here = jnp.concatenate([own_ref[0], own_ref[1]], axis=1)
        along = lax.dot_general(here, diff, NN, preferred_element_type=F32)
        lon = lon_ref[x : x + 1, :]
        lat = lat_ref[x : x + 1, :]
        flow = []
        for f in range(2):
            own = along[:, f * width_y : (f + 1) * width_y]
            at = f * half + x
            own = own - jnp.where(column_lane == 0, below[:, at : at + 1], 0.0)
            own = own + jnp.where(column_lane == width_y - 1, above[:, at : at + 1], 0.0)
            flow.append(own)
        across_u = east[0].astype(F32) - west[0].astype(F32)
        across_v = east[1].astype(F32) - west[1].astype(F32)
        ends_ref[end, :days, :] = (lon * across_v - lat * flow[0]).astype(BF16)
        ends_ref[end, days:, :] = (lon * across_u + lat * flow[1]).astype(BF16)

    fill = jnp.zeros((width_y - width_x, width_y), F32)
    lon_turned = jnp.concatenate([lon_ref[...], fill], axis=0).T
    lat_turned = jnp.concatenate([lat_ref[...], fill], axis=0).T
    spot = lane % half
    between = (spot > 0) & (spot < width_x - 1)
    parts = []
    for y, row, low, high in (
        (0, south_ref, below, second_ref[...].astype(F32)),
        (width_y - 1, north_ref, before_ref[...].astype(F32), above),
    ):
        lon = lon_turned[y : y + 1, :]
        lat = lat_turned[y : y + 1, :]
        lon = jnp.where(between, jnp.where(lane < half, lon, pltpu.roll(lon, half, 1)), 0.0)
        lat = jnp.where(between, jnp.where(lane < half, -lat, pltpu.roll(lat, half, 1)), 0.0)
        own = row[...].astype(F32)
        across = pltpu.roll(own, width_y - 1, 1) - pltpu.roll(own, 1, 1)
        parts.append(lon * pltpu.roll(across, half, 1) + lat * (high - low))
    low_lane = column_lane < half
    rows_ref[:days, :] = jnp.where(low_lane, parts[0], pltpu.roll(parts[1], half, 1)).astype(BF16)
    rows_ref[days:, :] = jnp.where(low_lane, pltpu.roll(parts[0], half, 1), parts[1]).astype(BF16)

    rim = jnp.concatenate([ends_ref[0], ends_ref[1], rows_ref[...]], axis=1)
    upper, lower = gram_of(rim, days)
    size = gram_ref.shape[1]
    at = 0
    for i in range(2 * days // size):
        for j in range(i, 2 * days // size):
            left = slice(i * size, (i + 1) * size)
            right = slice(j * size, (j + 1) * size)
            if i * size < days:
                extra = upper[left, right]
            else:
                extra = lower[
                    i * size - days : (i + 1) * size - days, j * size - days : (j + 1) * size - days
                ]
            gram_ref[at] = total_ref[left, right] + extra
            at += 1


def rim(ends, sides, edges, lon, lat, total, size):
    _, days, width_y = ends[0].shape
    count = 2 * days // size
    vmem = pl.BlockSpec(memory_space=pltpu.VMEM)
    operands = (*ends, *sides, *edges, lon, lat, total)
    return pl.pallas_call(
        rim_kernel,
        in_specs=[vmem] * len(operands),
        out_specs=[vmem] * 3,
        out_shape=[
            jax.ShapeDtypeStruct((count * (count + 1) // 2, size, size), F32),
            jax.ShapeDtypeStruct((2 * days, width_y), BF16),
            jax.ShapeDtypeStruct((2, 2 * days, width_y), BF16),
        ],
        compiler_params=pltpu.CompilerParams(vmem_limit_bytes=ROOM),
        name="rim",
    )(*operands)


def all_sum(x, beside):
    moves = []
    for axis in ("lat", "lon"):
        count = lax.axis_size(axis)
        assert count & (count - 1) == 0
        for bit in range(count.bit_length() - 1):
            moves.append((axis, bit))
    shape = x.shape
    x = x.reshape(-1, shape[-1])
    taken = []

    hops = 0

    def swap(block, axis, bit):
        nonlocal hops
        other = lax.ppermute(
            block, axis, [(i, i ^ 1 << bit) for i in range(lax.axis_size(axis))]
        )
        if hops in beside:
            other = other + beside[hops](block)[0, 0]
        hops += 1
        return other

    for axis, bit in moves:
        halve = x.shape[0] % 16 == 0 and x.shape[0] > shape[0] * 16
        if halve:
            half = x.shape[0] // 2
            high = (lax.axis_index(axis) >> bit) & 1
            keep = lax.dynamic_slice_in_dim(x, high * half, half, 0)
            send = lax.dynamic_slice_in_dim(x, (1 - high) * half, half, 0)
            x = keep + swap(send, axis, bit)
        else:
            x = x + swap(x, axis, bit)
        taken.append(halve)
    for (axis, bit), halve in reversed(list(zip(moves, taken))):
        if halve:
            high = (lax.axis_index(axis) >> bit) & 1
            other = swap(x, axis, bit)
            x = jnp.where(
                high == 1, jnp.concatenate([other, x], 0), jnp.concatenate([x, other], 0)
            )
    return x.reshape(shape)


def pick_kernel(
    piece, share, index_hbm, fields_hbm, rim_ref, ends_ref, after_ref, out_hbm, token_ref,
    index_ref, stage, rows, picked, turned_out, sems, out_sems,
):
    token_ref[...] = jnp.zeros_like(token_ref)
    columns, wide = rim_ref.shape
    count = out_hbm.shape[0]
    cells = fields_hbm.shape[1]
    width_x = cells // wide
    parts = columns // 128
    chunk = stage.shape[2]

    def fetch(i):
        return pltpu.make_async_copy(
            fields_hbm.at[:, i * chunk : (i + 1) * chunk], stage.at[i], sems.at[i]
        )

    places = pltpu.make_async_copy(index_hbm, index_ref, out_sems.at[2])
    places.start()
    for i in range(cells // chunk):
        fetch(i).start()
    unit = jnp.where(iota((wide, wide), 0) == iota((wide, wide), 1), 1.0, 0.0).astype(BF16)

    def turned(block):
        return lax.dot_general(unit, block, NT, preferred_element_type=F32)

    rim = turned(rim_ref[...])
    for i in range(cells // chunk):
        fetch(i).wait()
        for x in range(i * chunk // wide, (i + 1) * chunk // wide):
            at = x * wide * parts
            last = x == width_x - 1
            inside = x > 0 and not last
            if inside:
                start = x * wide - i * chunk
                block = turned(stage[i, :, start : start + wide])
            else:
                block = turned(ends_ref[int(last)])
            for c in range(parts):
                own = slice(c * 128, (c + 1) * 128)
                rows[pl.ds(at + c, wide, stride=parts), :] = block[:, own]
                if inside:
                    rows[at + c : at + c + 1, :] = rim[x : x + 1, own]
                    end = at + (wide - 1) * parts + c
                    rows[end : end + 1, :] = rim[wide // 2 + x : wide // 2 + x + 1, own]

    places.wait()
    block = turned_out.shape[1]

    def row(at):
        return rows[pl.ds(pl.multiple_of(index_ref[at], parts), parts), :]

    def send(i):
        return pltpu.make_async_copy(
            turned_out.at[i % 2], out_hbm.at[i * block : (i + 1) * block], out_sems.at[i % 2]
        )

    for i in range(count // block):
        if i >= 2:
            send(i - 2).wait()

        def body(k, _):
            start = k * share
            slot = lax.rem(k, 2)
            source = piece * count + i * block + start
            for j in range(0, share, 2):
                pair = jnp.concatenate([row(source + j), row(source + j + 1)], axis=0)
                picked[slot, j * parts : (j + 2) * parts, :] = pair
            for c in range(parts):
                part = picked[slot, pl.ds(c, share, stride=parts), :]
                turned_out[
                    i % 2, pl.ds(pl.multiple_of(start, share), share), c * 128 : (c + 1) * 128
                ] = part.astype(BF16)
            return 0

        lax.fori_loop(0, block // share, body, 0)
        send(i).start()
    for i in range(max(count // block - 2, 0), count // block):
        send(i).wait()


def pick(piece, pieces, places, fields, rim, ends, after):
    columns, cells = fields.shape
    wide = rim.shape[1]
    parts = columns // 128
    share = 64
    block = next(n for n in (768, 512, 256, 128, 64) if cells % (pieces * n) == 0)
    chunk = next(n * wide for n in (8, 6, 4, 3, 2, 1) if cells % (n * wide) == 0)
    vmem = pl.BlockSpec(memory_space=pltpu.VMEM)
    hbm = pl.BlockSpec(memory_space=pl.ANY)
    return pl.pallas_call(
        functools.partial(pick_kernel, piece, share),
        in_specs=[hbm, hbm, vmem, vmem, hbm],
        out_specs=[hbm, vmem],
        out_shape=[jax.ShapeDtypeStruct((cells // pieces, columns), BF16), TOKEN],
        scratch_shapes=[
            pltpu.SMEM((cells,), jnp.int32),
            pltpu.VMEM((cells // chunk, columns, chunk), BF16),
            pltpu.VMEM((cells * parts + 8, 128), F32),
            pltpu.VMEM((2, share * parts + 8, 128), F32),
            pltpu.VMEM((2, block, columns), BF16),
            pltpu.SemaphoreType.DMA((cells // chunk,)),
            pltpu.SemaphoreType.DMA((3,)),
        ],
        compiler_params=pltpu.CompilerParams(vmem_limit_bytes=50 * MB),
        name="pick",
    )(places, fields, rim, ends, after)


def sublane(x, t):
    return jnp.broadcast_to(x[t : t + 1, :], x.shape)


def lane_of(x, t):
    at = jnp.full(x.shape, t, jnp.int32)
    return jnp.take_along_axis(x, at, axis=1, mode="promise_in_bounds")


def thirds(x):
    high = x.astype(BF16).astype(F32)
    rest = x - high
    middle = rest.astype(BF16).astype(F32)
    return high, middle, rest - middle


def eliminate(work, head, row):
    head = list(head)
    done = jnp.zeros_like(work)
    pivots = jnp.ones_like(work)
    for t in range(0, 8, 2):
        one, two = row == t, row == t + 1
        both = one | two
        a, b, c = sublane(head[t], t), sublane(head[t + 1], t), sublane(head[t + 1], t + 1)
        determinant = a * c - b * b
        inverse = 1.0 / determinant
        first = jnp.where(one, c, jnp.where(two, -b, head[t + 1] * b - head[t] * c))
        second = jnp.where(one, -b, jnp.where(two, a, head[t] * b - head[t + 1] * a))

        def apply(x):
            step = first * sublane(x, t) + second * sublane(x, t + 1)
            return jnp.where(both, 0.0, x) + step * inverse

        share = 1.0 / a
        upper, lower = sublane(work, t), sublane(work, t + 1)
        done = jnp.where(one, upper, jnp.where(two, lower - b * share * upper, done))
        pivots = jnp.where(one, a, jnp.where(two, determinant * share, pivots))
        for u in range(t + 2, 8):
            head[u] = apply(head[u])
        work = apply(work)
    return work, done, pivots


def inverse_factor(block, near=1):
    size = block.shape[0]
    count = size // 8
    lane = iota((8, size), 1)
    row = iota((8, size), 0)
    tiles = [block[8 * p : 8 * p + 8, :] for p in range(count)]
    out = []
    for p in range(count):
        base = 8 * p
        close = range(p + 1, min(p + 1 + near, count))
        cols = {q: [lane_of(tiles[q], base + t) for t in range(8)] for q in (p, *close)}
        own = (lane >= base) & (lane < base + 8)
        unit = jnp.where(lane == base + row, 1.0, 0.0)
        work, done, pivots = eliminate(jnp.where(own, unit, tiles[p]), cols[p], row)
        out.append(jnp.where(lane <= base + row, done * lax.rsqrt(pivots), 0.0))
        lines = [sublane(work, t) for t in range(8)]
        for q in close:
            terms = [cols[q][t] * lines[t] for t in range(8)]
            while len(terms) > 1:
                terms = [terms[i] + terms[i + 1] for i in range(0, len(terms), 2)]
            tiles[q] = jnp.where(own, 0.0, tiles[q]) - terms[0]
        if p + 1 + near < count:
            ah, am, al = thirds(jnp.where(lane >= base + 8 * (1 + near), tiles[p], 0.0))
            wh, wm, wl = thirds(work)
            left = jnp.concatenate([ah, ah, am, ah, al, am], axis=0).astype(BF16)
            right = jnp.concatenate([wh, wm, wh, wl, wh, wm], axis=0).astype(BF16)
            change = lax.dot_general(left, right, TN, preferred_element_type=F32)
            for q in range(p + 1 + near, count):
                tiles[q] = jnp.where(own, 0.0, tiles[q]) - change[8 * q : 8 * q + 8, :]
    return jnp.concatenate(out, axis=0)


def factor_kernel(
    scale, pieces_ref, rows_hbm, r_ref, basis_hbm, work, high_ref, low_ref, rows, stage, lead, sems
):
    columns = r_ref.shape[0]
    chunks, _, width = stage.shape[0], columns, stage.shape[2]
    steps = rows.shape[0] // width
    fetch = pltpu.make_async_copy(rows_hbm, rows, sems.at[chunks])
    fetch.start()
    opening = pltpu.make_async_copy(pieces_ref.at[0], lead, sems.at[chunks + 1])
    opening.start()
    opening.wait()
    size = pieces_ref.shape[1]
    count = columns // size
    same = iota((size, size), 0) == iota((size, size), 1)
    upper = iota((size, size), 0) <= iota((size, size), 1)

    def dot(a, b, dims):
        return lax.dot_general(
            a, b, dims, preferred_element_type=F32, precision=lax.Precision.HIGHEST
        )

    def piece(at):
        return pieces_ref[at] if at else lead[...]

    order = [(i, j) for i in range(count) for j in range(i, count)]
    across, along = [], []
    for i in range(count):
        diagonal = jnp.where(same, piece(order.index((i, i))), 0.0)
        across.append(lax.rsqrt(jnp.sum(diagonal, axis=0, keepdims=True)))
        along.append(lax.rsqrt(jnp.sum(diagonal, axis=1, keepdims=True)))
    for at, (i, j) in enumerate(order):
        work[i, j] = piece(at) * along[i] * across[j]

    def place(i, j):
        return slice(i * size, (i + 1) * size), slice(j * size, (j + 1) * size)

    for k in range(count):
        diagonal = work[k, k]
        inverse = inverse_factor(diagonal)
        for j in (*range(k + 1, count), *range(k)):
            work[k, j] = dot(inverse, work[k, j], NN)
        work[k, k] = inverse
        for i in range(k + 1, count):
            left = work[k, i]
            for j in (*range(i, count), *range(k + 1)):
                change = dot(left, work[k, j], TN)
                work[i, j] = -change if j == k else work[i, j] - change
        corner = jnp.where(upper, dot(inverse, diagonal, NN), 0.0)
        for j in range(count):
            known = work[k, j] * (across[j] * scale) if j <= k else jnp.zeros((size, size), F32)
            high = known.astype(BF16)
            high_ref[place(k, j)] = high
            low_ref[place(k, j)] = (known - high.astype(F32)).astype(BF16)
            grow = 1.0 / (across[j] * scale)
            r_ref[place(k, j)] = (
                corner * grow if j == k else work[k, j] * grow if j > k else jnp.zeros((size, size), F32)
            )

    fetch.wait()
    half = columns // 2

    def product(w, x):
        return lax.dot_general(w, x, NT, preferred_element_type=F32)

    def send(i):
        slot = lax.rem(i, chunks)
        place = pl.ds(pl.multiple_of(i * width, width), width)
        return pltpu.make_async_copy(stage.at[slot], basis_hbm.at[:, place], sems.at[slot])

    def body(i, _):
        slot = lax.rem(i, chunks)

        @pl.when(i >= chunks)
        def _():
            send(i - chunks).wait()

        block = rows[pl.ds(pl.multiple_of(i * width, width), width), :]
        first = block[:, :half]
        top = product(low_ref[:half, :half], first) + product(high_ref[:half, :half], first)
        stage[slot, :half, :] = top.astype(BF16)
        bottom = product(low_ref[half:, :], block) + product(high_ref[half:, :], block)
        stage[slot, half:, :] = bottom.astype(BF16)
        send(i).start()
        return 0

    lax.fori_loop(0, steps, body, 0)
    for i in range(max(steps - chunks, 0), steps):
        send(i).wait()


def factor(pieces, rows, columns, scale):
    vmem = pl.BlockSpec(memory_space=pltpu.VMEM)
    hbm = pl.BlockSpec(memory_space=pl.ANY)
    square = (columns, columns)
    size = pieces.shape[1]
    cells = rows.shape[0]
    width = next(n for n in (1536, 768, 512, 256, 128) if cells % n == 0)
    chunks = min(3, cells // width)
    return pl.pallas_call(
        functools.partial(factor_kernel, scale),
        in_specs=[vmem, hbm],
        out_specs=[vmem, hbm],
        out_shape=[
            jax.ShapeDtypeStruct(square, F32),
            jax.ShapeDtypeStruct((columns, cells), BF16),
        ],
        scratch_shapes=[
            pltpu.VMEM((columns // size, columns // size, size, size), F32),
            pltpu.VMEM(square, BF16),
            pltpu.VMEM(square, BF16),
            pltpu.VMEM((cells, columns), BF16),
            pltpu.VMEM((chunks, columns, width), BF16),
            pltpu.VMEM((size, size), F32),
            pltpu.SemaphoreType.DMA((chunks + 2,)),
        ],
        compiler_params=pltpu.CompilerParams(vmem_limit_bytes=50 * MB),
        name="factor",
    )(pieces, rows)


def shards(velocity, lon_metric, lat_metric, wet_index, wet_count):
    days = velocity.shape[1]
    cells = velocity.shape[2] * velocity.shape[3]
    columns = 2 * days
    lats, lons = lax.axis_size("lat"), lax.axis_size("lon")
    row = lax.axis_index("lat")
    flag = (row % 2 + 2 * (row == lats - 1)).astype(F32)
    fields, total, lon, lat, south, second, north, before, near, far, *outer, flag = front(
        velocity, wet_index, wet_count, lon_metric, lat_metric, flag
    )
    east_route = [(i, (i + 1) % lons) for i in range(lons)]
    west = lax.ppermute(outer[3], "lon", east_route)
    east = lax.ppermute(outer[0], "lon", [(t, s) for s, t in east_route])
    assert lats % 2 == 0
    near = lax.ppermute(near, "lat", [(i, i ^ 1) for i in range(lats)])
    route = []
    for x in range(lons):
        for y in range(1, lats - 1):
            other = y + 1 if y % 2 else y - 1
            route.append((y * lons + x, other * lons + x))
        route.append(((lats - 1) * lons + x, lats * lons - 1 - x))
    far = lax.ppermute(far, ("lat", "lon"), route)
    sides = (west, east, near, far, flag)
    cells_in_order, lon = lax.optimization_barrier((wet_index, lon))
    places = cells_in_order * (columns // 128)
    edges = (south, second, north, before)
    gram, rows, ends = rim(outer, sides, edges, lon, lat, total, min(128, columns))

    pieces = 1
    held = {}

    def picking(piece, after):
        held[piece], token = pick(piece, pieces, places, fields, rows, ends, after)
        return token

    beside = {1 + piece: functools.partial(picking, piece) for piece in range(pieces)}
    total = all_sum(gram, beside)
    scale = math.sqrt(cells * lats * lons)
    triangle, basis = factor(total, held[0], columns, scale)
    return basis, triangle


def solution(mesh):
    placed = (
        P(None, None, "lon", "lat"),
        P("lon", "lat"),
        P("lon", "lat"),
        P(("lat", "lon")),
        P(("lat", "lon")),
    )
    return jax.shard_map(
        shards,
        mesh=mesh,
        in_specs=placed,
        out_specs=(P(None, ("lat", "lon")), P()),
        check_vma=False,
    )
```

```python
import functools
import math

import jax
import jax.numpy as jnp
from jax import lax
from jax.experimental import pallas as pl
from jax.experimental.pallas import tpu as pltpu
from jax.sharding import PartitionSpec as P

F32 = jnp.float32
BF16 = jnp.bfloat16
MB = 1 << 20
ROOM = 24 * MB
TOKEN = jax.ShapeDtypeStruct((8, 128), F32)
NN = (((1,), (0,)), ((), ()))
NT = (((1,), (1,)), ((), ()))
TN = (((0,), (0,)), ((), ()))


def iota(shape, dim):
    return lax.broadcasted_iota(jnp.int32, shape, dim)


def lat_difference(width_y):
    wide = 2 * width_y
    k = iota((wide, wide), 0)
    n = iota((wide, wide), 1)
    same = k // width_y == n // width_y
    diff = jnp.where(same & (k == n + 1), 1.0, 0.0) - jnp.where(same & (k == n - 1), 1.0, 0.0)
    return diff.astype(BF16)


def gram_of(block, days):
    upper = lax.dot_general(block[:days, :], block, NT, preferred_element_type=F32)
    lower = lax.dot_general(block[days:, :], block[days:, :], NT, preferred_element_type=F32)
    return upper, lower


def front_kernel(
    v_hbm, cells_ref, count_ref,
    fields_hbm, total, lon_out, lat_out, south_ref, second_ref, north_ref, before_ref, near_ref, far_ref,
    x0_ref, x1_ref, x2_ref, x3_ref, flag_ref,
    raw, moved, stage, lon_in, lat_in, sems, out_sems,
):
    fields, days, width_x, width_y = v_hbm.shape
    step = raw.shape[2]
    half = width_y // 2

    def fetch(i):
        return pltpu.make_async_copy(
            v_hbm.at[:, pl.ds(i * step, step)], raw.at[i], sems.at[i]
        )

    for i in range(days // step):
        fetch(i).start()

    cells = width_x * width_y
    index = cells_ref[2].astype(jnp.int32)
    index = jnp.concatenate([index[x : x + 1, :] for x in range(width_x)], axis=1)
    wet = iota(index.shape, 1) < count_ref[0]
    row = jnp.where(wet, index // width_y, -1)
    col = index % width_y
    pick_x = jnp.where(iota((width_x, cells), 0) == row, 1.0, 0.0).astype(BF16)
    pick_y = jnp.where(iota((width_y, cells), 0) == col, 1.0, 0.0).astype(BF16)
    mask = lax.dot_general(pick_x, pick_y, NT, preferred_element_type=F32)
    at_x = iota((width_x, width_y), 0)
    at_y = iota((width_x, width_y), 1)
    inner = (at_x > 0) & (at_x < width_x - 1) & (at_y > 0) & (at_y < width_y - 1)
    lon = 0.5 * cells_ref[0] * mask
    lat = 0.5 * cells_ref[1] * mask
    lon_out[...] = lon
    lat_out[...] = lat
    lon_in[...] = jnp.where(inner, lon, 0.0)
    lat_in[...] = jnp.where(inner, lat, 0.0)

    lane = iota((16, width_y), 1)

    def turn(i, _):
        fetch(i).wait()
        for d in range(0, step, 16):
            south = second = north = before = jnp.zeros((16, width_y), BF16)
            rows = pl.ds(pl.multiple_of(i * step + d, 16), 16)
            for f in range(fields):
                columns = jnp.swapaxes(raw[i, f, d : d + 16], 0, 1)
                moved[f, :, rows, :] = columns
                for x in range(width_x):
                    at = f * half + x
                    turned = pltpu.roll(columns[x], at + 1, 1)
                    before = jnp.where(lane == (at - 1) % width_y, turned, before)
                    north = jnp.where(lane == at, turned, north)
                    south = jnp.where(lane == at + 1, turned, south)
                    second = jnp.where(lane == at + 2, turned, second)
            south_ref[rows, :] = pltpu.roll(south, width_y - 1, 1)
            second_ref[rows, :] = pltpu.roll(second, width_y - 2, 1)
            north_ref[rows, :] = north
            before_ref[rows, :] = pltpu.roll(before, 1, 1)
        return 0

    lax.fori_loop(0, days // step, turn, 0)
    k = iota((width_y, width_y), 0)
    n = iota((width_y, width_y), 1)
    mirror = (k // half == n // half) & (k + n == 2 * half * (n // half) + width_x - 1)
    mirror = jnp.where(mirror, -1.0, 0.0).astype(BF16)
    fold = lax.dot_general(north_ref[...], mirror, NN, preferred_element_type=F32)
    flag = cells_ref[3, :1, :]
    flag_ref[...] = cells_ref[3, :8, :]
    odd, top = flag % 2 == 1, flag >= 2
    south, north = south_ref[...].astype(F32), north_ref[...].astype(F32)
    near_ref[...] = jnp.where(odd, south, north).astype(BF16)
    far_ref[...] = jnp.where(top, fold, jnp.where(odd, north, south)).astype(BF16)
    x0_ref[...] = moved[:, 0]
    x1_ref[...] = moved[:, 1]
    x2_ref[...] = moved[:, width_x - 2]
    x3_ref[...] = moved[:, width_x - 1]

    wide = stage.shape[2]
    group = wide // width_y
    steps = width_x // group
    diff = lat_difference(width_y)
    total[...] = jnp.zeros_like(total)

    def send(i):
        slot = lax.rem(i, 2)
        place = pl.ds(pl.multiple_of(i * wide, wide), wide)
        return pltpu.make_async_copy(stage.at[slot], fields_hbm.at[:, place], out_sems.at[slot])

    def compute(i, _):
        slot = lax.rem(i, 2)

        @pl.when(i >= 2)
        def _():
            send(i - 2).wait()

        for g in range(group):
            x = i * group + g
            east = jnp.minimum(x + 1, width_x - 1)
            west = jnp.maximum(x - 1, 0)
            here = jnp.concatenate([moved[0, x], moved[1, x]], axis=1)
            along = lax.dot_general(here, diff, NN, preferred_element_type=F32)
            lon = lon_in[pl.ds(x, 1), :]
            lat = lat_in[pl.ds(x, 1), :]
            across_u = moved[0, east].astype(F32) - moved[0, west].astype(F32)
            across_v = moved[1, east].astype(F32) - moved[1, west].astype(F32)
            zeta = lon * across_v - lat * along[:, :width_y]
            divergence = lon * across_u + lat * along[:, width_y:]
            place = slice(g * width_y, (g + 1) * width_y)
            stage[slot, :days, place] = zeta.astype(BF16)
            stage[slot, days:, place] = divergence.astype(BF16)
        send(i).start()
        upper, lower = gram_of(stage[slot], days)
        total[:days, :] += upper
        total[days:, days:] += lower
        return 0

    lax.fori_loop(0, steps, compute, 0)
    for i in range(max(steps - 2, 0), steps):
        send(i).wait()


def front(velocity, wet_index, wet_count, lon_metric, lat_metric, flag):
    fields, days, width_x, width_y = velocity.shape
    assert width_x <= width_y // 2 - 2
    step = next(n for n in (32, 16) if days % n == 0)
    places = wet_index.reshape(width_x, width_y).astype(F32)
    group = next(n for n in (16, 8, 6, 4, 3, 2, 1) if width_x % n == 0)
    vmem = pl.BlockSpec(memory_space=pltpu.VMEM)
    hbm = pl.BlockSpec(memory_space=pl.ANY)
    metric = jax.ShapeDtypeStruct((width_x, width_y), F32)
    edge = jax.ShapeDtypeStruct((days, width_y), BF16)
    column = jax.ShapeDtypeStruct((fields, days, width_y), BF16)
    return pl.pallas_call(
        front_kernel,
        in_specs=[hbm, vmem, pl.BlockSpec(memory_space=pltpu.SMEM)],
        out_specs=[hbm] + [vmem] * 14,
        out_shape=[
            jax.ShapeDtypeStruct((2 * days, width_x * width_y), BF16),
            jax.ShapeDtypeStruct((2 * days, 2 * days), F32),
            metric, metric, *[edge] * 6, *[column] * 4, jax.ShapeDtypeStruct((8, width_y), F32),
        ],
        scratch_shapes=[
            pltpu.VMEM((days // step, fields, step, width_x, width_y), BF16),
            pltpu.VMEM((fields, width_x, days, width_y), BF16),
            pltpu.VMEM((2, 2 * days, group * width_y), BF16),
            pltpu.VMEM((width_x, width_y), F32),
            pltpu.VMEM((width_x, width_y), F32),
            pltpu.SemaphoreType.DMA((days // step,)),
            pltpu.SemaphoreType.DMA((2,)),
        ],
        compiler_params=pltpu.CompilerParams(vmem_limit_bytes=50 * MB),
        name="front",
    )(velocity, jnp.stack([lon_metric, lat_metric, places, jnp.full_like(places, flag)]), wet_count)


def rim_kernel(
    x0_ref, x1_ref, x2_ref, x3_ref, west_ref, east_ref, near_ref, far_ref, flag_ref,
    south_ref, second_ref, north_ref, before_ref, lon_ref, lat_ref, total_ref,
    gram_ref, rows_ref, ends_ref,
):
    _, days, width_y = x0_ref.shape
    width_x = lon_ref.shape[0]
    half = width_y // 2
    odd = flag_ref[:1, :] % 2 == 1
    near, far = near_ref[...].astype(F32), far_ref[...].astype(F32)
    below, above = jnp.where(odd, near, far), jnp.where(odd, far, near)
    lane = iota((1, width_y), 1)

    diff = lat_difference(width_y)
    column_lane = iota((days, width_y), 1)
    for end, x, own_ref, west, east in (
        (0, 0, x0_ref, west_ref, x1_ref),
        (1, width_x - 1, x3_ref, x2_ref, east_ref),
    ):
        here = jnp.concatenate([own_ref[0], own_ref[1]], axis=1)
        along = lax.dot_general(here, diff, NN, preferred_element_type=F32)
        lon = lon_ref[x : x + 1, :]
        lat = lat_ref[x : x + 1, :]
        flow = []
        for f in range(2):
            own = along[:, f * width_y : (f + 1) * width_y]
            at = f * half + x
            own = own - jnp.where(column_lane == 0, below[:, at : at + 1], 0.0)
            own = own + jnp.where(column_lane == width_y - 1, above[:, at : at + 1], 0.0)
            flow.append(own)
        across_u = east[0].astype(F32) - west[0].astype(F32)
        across_v = east[1].astype(F32) - west[1].astype(F32)
        ends_ref[end, :days, :] = (lon * across_v - lat * flow[0]).astype(BF16)
        ends_ref[end, days:, :] = (lon * across_u + lat * flow[1]).astype(BF16)

    fill = jnp.zeros((width_y - width_x, width_y), F32)
    lon_turned = jnp.concatenate([lon_ref[...], fill], axis=0).T
    lat_turned = jnp.concatenate([lat_ref[...], fill], axis=0).T
    spot = lane % half
    between = (spot > 0) & (spot < width_x - 1)
    parts = []
    for y, row, low, high in (
        (0, south_ref, below, second_ref[...].astype(F32)),
        (width_y - 1, north_ref, before_ref[...].astype(F32), above),
    ):
        lon = lon_turned[y : y + 1, :]
        lat = lat_turned[y : y + 1, :]
        lon = jnp.where(between, jnp.where(lane < half, lon, pltpu.roll(lon, half, 1)), 0.0)
        lat = jnp.where(between, jnp.where(lane < half, -lat, pltpu.roll(lat, half, 1)), 0.0)
        own = row[...].astype(F32)
        across = pltpu.roll(own, width_y - 1, 1) - pltpu.roll(own, 1, 1)
        parts.append(lon * pltpu.roll(across, half, 1) + lat * (high - low))
    low_lane = column_lane < half
    rows_ref[:days, :] = jnp.where(low_lane, parts[0], pltpu.roll(parts[1], half, 1)).astype(BF16)
    rows_ref[days:, :] = jnp.where(low_lane, pltpu.roll(parts[0], half, 1), parts[1]).astype(BF16)

    rim = jnp.concatenate([ends_ref[0], ends_ref[1], rows_ref[...]], axis=1)
    upper, lower = gram_of(rim, days)
    size = gram_ref.shape[1]
    at = 0
    for i in range(2 * days // size):
        for j in range(i, 2 * days // size):
            left = slice(i * size, (i + 1) * size)
            right = slice(j * size, (j + 1) * size)
            if i * size < days:
                extra = upper[left, right]
            else:
                extra = lower[
                    i * size - days : (i + 1) * size - days, j * size - days : (j + 1) * size - days
                ]
            gram_ref[at] = total_ref[left, right] + extra
            at += 1


def rim(ends, sides, edges, lon, lat, total, size):
    _, days, width_y = ends[0].shape
    count = 2 * days // size
    vmem = pl.BlockSpec(memory_space=pltpu.VMEM)
    operands = (*ends, *sides, *edges, lon, lat, total)
    return pl.pallas_call(
        rim_kernel,
        in_specs=[vmem] * len(operands),
        out_specs=[vmem] * 3,
        out_shape=[
            jax.ShapeDtypeStruct((count * (count + 1) // 2, size, size), F32),
            jax.ShapeDtypeStruct((2 * days, width_y), BF16),
            jax.ShapeDtypeStruct((2, 2 * days, width_y), BF16),
        ],
        compiler_params=pltpu.CompilerParams(vmem_limit_bytes=ROOM),
        name="rim",
    )(*operands)


def all_sum(x, beside):
    moves = []
    for axis in ("lat", "lon"):
        count = lax.axis_size(axis)
        assert count & (count - 1) == 0
        for bit in range(count.bit_length() - 1):
            moves.append((axis, bit))
    shape = x.shape
    x = x.reshape(-1, shape[-1])
    taken = []

    hops = 0

    def swap(block, axis, bit):
        nonlocal hops
        other = lax.ppermute(
            block, axis, [(i, i ^ 1 << bit) for i in range(lax.axis_size(axis))]
        )
        if hops in beside:
            other = other + beside[hops](block)[0, 0]
        hops += 1
        return other

    for axis, bit in moves:
        halve = x.shape[0] % 16 == 0 and x.shape[0] > shape[0] * 16
        if halve:
            half = x.shape[0] // 2
            high = (lax.axis_index(axis) >> bit) & 1
            keep = lax.dynamic_slice_in_dim(x, high * half, half, 0)
            send = lax.dynamic_slice_in_dim(x, (1 - high) * half, half, 0)
            x = keep + swap(send, axis, bit)
        else:
            x = x + swap(x, axis, bit)
        taken.append(halve)
    for (axis, bit), halve in reversed(list(zip(moves, taken))):
        if halve:
            high = (lax.axis_index(axis) >> bit) & 1
            other = swap(x, axis, bit)
            x = jnp.where(
                high == 1, jnp.concatenate([other, x], 0), jnp.concatenate([x, other], 0)
            )
    return x.reshape(shape)


def pick_kernel(
    piece, share, index_hbm, fields_hbm, rim_ref, ends_ref, after_ref, out_hbm, token_ref,
    index_ref, stage, rows, picked, turned_out, sems, out_sems,
):
    token_ref[...] = jnp.zeros_like(token_ref)
    columns, wide = rim_ref.shape
    count = out_hbm.shape[0]
    cells = fields_hbm.shape[1]
    width_x = cells // wide
    parts = columns // 128
    chunk = stage.shape[2]

    def fetch(i):
        return pltpu.make_async_copy(
            fields_hbm.at[:, i * chunk : (i + 1) * chunk], stage.at[i], sems.at[i]
        )

    places = pltpu.make_async_copy(index_hbm, index_ref, out_sems.at[2])
    places.start()
    for i in range(cells // chunk):
        fetch(i).start()
    unit = jnp.where(iota((wide, wide), 0) == iota((wide, wide), 1), 1.0, 0.0).astype(BF16)

    def turned(block):
        return lax.dot_general(unit, block, NT, preferred_element_type=F32)

    rim = turned(rim_ref[...])
    for i in range(cells // chunk):
        fetch(i).wait()
        for x in range(i * chunk // wide, (i + 1) * chunk // wide):
            at = x * wide * parts
            last = x == width_x - 1
            inside = x > 0 and not last
            if inside:
                start = x * wide - i * chunk
                block = turned(stage[i, :, start : start + wide])
            else:
                block = turned(ends_ref[int(last)])
            for c in range(parts):
                own = slice(c * 128, (c + 1) * 128)
                rows[pl.ds(at + c, wide, stride=parts), :] = block[:, own]
                if inside:
                    rows[at + c : at + c + 1, :] = rim[x : x + 1, own]
                    end = at + (wide - 1) * parts + c
                    rows[end : end + 1, :] = rim[wide // 2 + x : wide // 2 + x + 1, own]

    places.wait()
    block = turned_out.shape[1]

    def row(at):
        return rows[pl.ds(pl.multiple_of(index_ref[at], parts), parts), :]

    def send(i):
        return pltpu.make_async_copy(
            turned_out.at[i % 2], out_hbm.at[i * block : (i + 1) * block], out_sems.at[i % 2]
        )

    for i in range(count // block):
        if i >= 2:
            send(i - 2).wait()

        def body(k, _):
            start = k * share
            slot = lax.rem(k, 2)
            source = piece * count + i * block + start
            for j in range(0, share, 2):
                pair = jnp.concatenate([row(source + j), row(source + j + 1)], axis=0)
                picked[slot, j * parts : (j + 2) * parts, :] = pair
            for c in range(parts):
                part = picked[slot, pl.ds(c, share, stride=parts), :]
                turned_out[
                    i % 2, pl.ds(pl.multiple_of(start, share), share), c * 128 : (c + 1) * 128
                ] = part.astype(BF16)
            return 0

        lax.fori_loop(0, block // share, body, 0)
        send(i).start()
    for i in range(max(count // block - 2, 0), count // block):
        send(i).wait()


def pick(piece, pieces, places, fields, rim, ends, after):
    columns, cells = fields.shape
    wide = rim.shape[1]
    parts = columns // 128
    share = 64
    block = next(n for n in (768, 512, 256, 128, 64) if cells % (pieces * n) == 0)
    chunk = next(n * wide for n in (8, 6, 4, 3, 2, 1) if cells % (n * wide) == 0)
    vmem = pl.BlockSpec(memory_space=pltpu.VMEM)
    hbm = pl.BlockSpec(memory_space=pl.ANY)
    return pl.pallas_call(
        functools.partial(pick_kernel, piece, share),
        in_specs=[hbm, hbm, vmem, vmem, hbm],
        out_specs=[hbm, vmem],
        out_shape=[jax.ShapeDtypeStruct((cells // pieces, columns), BF16), TOKEN],
        scratch_shapes=[
            pltpu.SMEM((cells,), jnp.int32),
            pltpu.VMEM((cells // chunk, columns, chunk), BF16),
            pltpu.VMEM((cells * parts + 8, 128), F32),
            pltpu.VMEM((2, share * parts + 8, 128), F32),
            pltpu.VMEM((2, block, columns), BF16),
            pltpu.SemaphoreType.DMA((cells // chunk,)),
            pltpu.SemaphoreType.DMA((3,)),
        ],
        compiler_params=pltpu.CompilerParams(vmem_limit_bytes=50 * MB),
        name="pick",
    )(places, fields, rim, ends, after)


def sublane(x, t):
    return jnp.broadcast_to(x[t : t + 1, :], x.shape)


def lane_of(x, t):
    at = jnp.full(x.shape, t, jnp.int32)
    return jnp.take_along_axis(x, at, axis=1, mode="promise_in_bounds")


def thirds(x):
    high = x.astype(BF16).astype(F32)
    rest = x - high
    middle = rest.astype(BF16).astype(F32)
    return high, middle, rest - middle


def eliminate(work, head, row):
    head = list(head)
    done = jnp.zeros_like(work)
    pivots = jnp.ones_like(work)
    for t in range(0, 8, 2):
        one, two = row == t, row == t + 1
        both = one | two
        a, b, c = sublane(head[t], t), sublane(head[t + 1], t), sublane(head[t + 1], t + 1)
        determinant = a * c - b * b
        inverse = 1.0 / determinant
        first = jnp.where(one, c, jnp.where(two, -b, head[t + 1] * b - head[t] * c))
        second = jnp.where(one, -b, jnp.where(two, a, head[t] * b - head[t + 1] * a))

        def apply(x):
            step = first * sublane(x, t) + second * sublane(x, t + 1)
            return jnp.where(both, 0.0, x) + step * inverse

        share = 1.0 / a
        upper, lower = sublane(work, t), sublane(work, t + 1)
        done = jnp.where(one, upper, jnp.where(two, lower - b * share * upper, done))
        pivots = jnp.where(one, a, jnp.where(two, determinant * share, pivots))
        for u in range(t + 2, 8):
            head[u] = apply(head[u])
        work = apply(work)
    return work, done, pivots


def inverse_factor(block, near=1):
    size = block.shape[0]
    count = size // 8
    lane = iota((8, size), 1)
    row = iota((8, size), 0)
    tiles = [block[8 * p : 8 * p + 8, :] for p in range(count)]
    out = []
    for p in range(count):
        base = 8 * p
        close = range(p + 1, min(p + 1 + near, count))
        cols = {q: [lane_of(tiles[q], base + t) for t in range(8)] for q in (p, *close)}
        own = (lane >= base) & (lane < base + 8)
        unit = jnp.where(lane == base + row, 1.0, 0.0)
        work, done, pivots = eliminate(jnp.where(own, unit, tiles[p]), cols[p], row)
        out.append(jnp.where(lane <= base + row, done * lax.rsqrt(pivots), 0.0))
        lines = [sublane(work, t) for t in range(8)]
        for q in close:
            terms = [cols[q][t] * lines[t] for t in range(8)]
            while len(terms) > 1:
                terms = [terms[i] + terms[i + 1] for i in range(0, len(terms), 2)]
            tiles[q] = jnp.where(own, 0.0, tiles[q]) - terms[0]
        if p + 1 + near < count:
            ah, am, al = thirds(jnp.where(lane >= base + 8 * (1 + near), tiles[p], 0.0))
            wh, wm, wl = thirds(work)
            left = jnp.concatenate([ah, ah, am, ah, al, am], axis=0).astype(BF16)
            right = jnp.concatenate([wh, wm, wh, wl, wh, wm], axis=0).astype(BF16)
            change = lax.dot_general(left, right, TN, preferred_element_type=F32)
            for q in range(p + 1 + near, count):
                tiles[q] = jnp.where(own, 0.0, tiles[q]) - change[8 * q : 8 * q + 8, :]
    return jnp.concatenate(out, axis=0)


def factor_kernel(
    scale, pieces_ref, rows_hbm, r_ref, basis_hbm, work, high_ref, low_ref, rows, stage, lead, sems
):
    columns = r_ref.shape[0]
    chunks, _, width = stage.shape[0], columns, stage.shape[2]
    steps = rows.shape[0] // width
    fetch = pltpu.make_async_copy(rows_hbm, rows, sems.at[chunks])
    fetch.start()
    opening = pltpu.make_async_copy(pieces_ref.at[0], lead, sems.at[chunks + 1])
    opening.start()
    opening.wait()
    size = pieces_ref.shape[1]
    count = columns // size
    same = iota((size, size), 0) == iota((size, size), 1)
    upper = iota((size, size), 0) <= iota((size, size), 1)

    def dot(a, b, dims):
        return lax.dot_general(
            a, b, dims, preferred_element_type=F32, precision=lax.Precision.HIGHEST
        )

    def piece(at):
        return pieces_ref[at] if at else lead[...]

    order = [(i, j) for i in range(count) for j in range(i, count)]
    across, along = [], []
    for i in range(count):
        diagonal = jnp.where(same, piece(order.index((i, i))), 0.0)
        across.append(lax.rsqrt(jnp.sum(diagonal, axis=0, keepdims=True)))
        along.append(lax.rsqrt(jnp.sum(diagonal, axis=1, keepdims=True)))
    for at, (i, j) in enumerate(order):
        work[i, j] = piece(at) * along[i] * across[j]

    def place(i, j):
        return slice(i * size, (i + 1) * size), slice(j * size, (j + 1) * size)

    for k in range(count):
        diagonal = work[k, k]
        inverse = inverse_factor(diagonal)
        for j in (*range(k + 1, count), *range(k)):
            work[k, j] = dot(inverse, work[k, j], NN)
        work[k, k] = inverse
        for i in range(k + 1, count):
            left = work[k, i]
            for j in (*range(i, count), *range(k + 1)):
                change = dot(left, work[k, j], TN)
                work[i, j] = -change if j == k else work[i, j] - change
        corner = jnp.where(upper, dot(inverse, diagonal, NN), 0.0)
        for j in range(count):
            known = work[k, j] * (across[j] * scale) if j <= k else jnp.zeros((size, size), F32)
            high = known.astype(BF16)
            high_ref[place(k, j)] = high
            low_ref[place(k, j)] = (known - high.astype(F32)).astype(BF16)
            grow = 1.0 / (across[j] * scale)
            r_ref[place(k, j)] = (
                corner * grow if j == k else work[k, j] * grow if j > k else jnp.zeros((size, size), F32)
            )

    fetch.wait()
    half = columns // 2

    def product(w, x):
        return lax.dot_general(w, x, NT, preferred_element_type=F32)

    def send(i):
        slot = lax.rem(i, chunks)
        place = pl.ds(pl.multiple_of(i * width, width), width)
        return pltpu.make_async_copy(stage.at[slot], basis_hbm.at[:, place], sems.at[slot])

    def body(i, _):
        slot = lax.rem(i, chunks)

        @pl.when(i >= chunks)
        def _():
            send(i - chunks).wait()

        block = rows[pl.ds(pl.multiple_of(i * width, width), width), :]
        first = block[:, :half]
        top = product(low_ref[:half, :half], first) + product(high_ref[:half, :half], first)
        stage[slot, :half, :] = top.astype(BF16)
        bottom = product(low_ref[half:, :], block) + product(high_ref[half:, :], block)
        stage[slot, half:, :] = bottom.astype(BF16)
        send(i).start()
        return 0

    lax.fori_loop(0, steps, body, 0)
    for i in range(max(steps - chunks, 0), steps):
        send(i).wait()


def factor(pieces, rows, columns, scale):
    vmem = pl.BlockSpec(memory_space=pltpu.VMEM)
    hbm = pl.BlockSpec(memory_space=pl.ANY)
    square = (columns, columns)
    size = pieces.shape[1]
    cells = rows.shape[0]
    width = next(n for n in (1536, 768, 512, 256, 128) if cells % n == 0)
    chunks = min(3, cells // width)
    return pl.pallas_call(
        functools.partial(factor_kernel, scale),
        in_specs=[vmem, hbm],
        out_specs=[vmem, hbm],
        out_shape=[
            jax.ShapeDtypeStruct(square, F32),
            jax.ShapeDtypeStruct((columns, cells), BF16),
        ],
        scratch_shapes=[
            pltpu.VMEM((columns // size, columns // size, size, size), F32),
            pltpu.VMEM(square, BF16),
            pltpu.VMEM(square, BF16),
            pltpu.VMEM((cells, columns), BF16),
            pltpu.VMEM((chunks, columns, width), BF16),
            pltpu.VMEM((size, size), F32),
            pltpu.SemaphoreType.DMA((chunks + 2,)),
        ],
        compiler_params=pltpu.CompilerParams(vmem_limit_bytes=50 * MB),
        name="factor",
    )(pieces, rows)


def shards(velocity, lon_metric, lat_metric, wet_index, wet_count):
    days = velocity.shape[1]
    cells = velocity.shape[2] * velocity.shape[3]
    columns = 2 * days
    lats, lons = lax.axis_size("lat"), lax.axis_size("lon")
    row = lax.axis_index("lat")
    flag = (row % 2 + 2 * (row == lats - 1)).astype(F32)
    fields, total, lon, lat, south, second, north, before, near, far, *outer, flag = front(
        velocity, wet_index, wet_count, lon_metric, lat_metric, flag
    )
    east_route = [(i, (i + 1) % lons) for i in range(lons)]
    west = lax.ppermute(outer[3], "lon", east_route)
    east = lax.ppermute(outer[0], "lon", [(t, s) for s, t in east_route])
    assert lats % 2 == 0
    near = lax.ppermute(near, "lat", [(i, i ^ 1) for i in range(lats)])
    route = []
    for x in range(lons):
        for y in range(1, lats - 1):
            other = y + 1 if y % 2 else y - 1
            route.append((y * lons + x, other * lons + x))
        route.append(((lats - 1) * lons + x, lats * lons - 1 - x))
    far = lax.ppermute(far, ("lat", "lon"), route)
    sides = (west, east, near, far, flag)
    cells_in_order, lon = lax.optimization_barrier((wet_index, lon))
    places = cells_in_order * (columns // 128)
    edges = (south, second, north, before)
    gram, rows, ends = rim(outer, sides, edges, lon, lat, total, min(128, columns))

    pieces = 1
    held = {}

    def picking(piece, after):
        held[piece], token = pick(piece, pieces, places, fields, rows, ends, after)
        return token

    beside = {1 + piece: functools.partial(picking, piece) for piece in range(pieces)}
    total = all_sum(gram, beside)
    scale = math.sqrt(cells * lats * lons)
    triangle, basis = factor(total, held[0], columns, scale)
    return basis, triangle


def solution(mesh):
    placed = (
        P(None, None, "lon", "lat"),
        P("lon", "lat"),
        P("lon", "lat"),
        P(("lat", "lon")),
        P(("lat", "lon")),
    )
    return jax.shard_map(
        shards,
        mesh=mesh,
        in_specs=placed,
        out_specs=(P(None, ("lat", "lon")), P()),
        check_vma=False,
    )
```
